256 devices in a mesh: replica: 16 (over z_hi, x), tensor: 16 (over z_lo, y, core).
Axes of the slice: x: 4, y: 4, z: 8 (z_hi: 4, z_lo: 2; z = z_hi * 2 + z_lo), core: 2. Of those that a mesh axis runs over, the one named last changes fastest.
Arguments:
- tokens: bfloat16 [16, 384, 2048], P('replica', 'tensor'), may hold values from -6 to 6
- targets: bfloat16 [16, 384, 2048], P('replica', 'tensor'), may hold values from -6 to 6
- gate_weight: bfloat16 [16, 2048, 7168], P('replica', None, 'tensor'), may hold values from -6 to 6
- probes: bfloat16 [16, 2048, 7168], P('replica', None, 'tensor'), may hold values from -6 to 6
- tracker: bfloat16 [16, 2048, 7168], P('replica', None, 'tensor'), may hold values from 0.049804688 to 2
- up_weight: bfloat16 [2048, 7168], P('replica', 'tensor'), may hold values from -6 to 6
- down_weight: bfloat16 [7168, 2048], P('tensor', 'replica'), may hold values from -6 to 6
- neighbours: int32 [16, 6], replicated, may hold values from 0 to 15, as said below
- numerators: int32 [16, 6], replicated, may hold values from 0 to 8, as said below
Outputs:
- mixed_weights: bfloat16 [16, 2048, 7168], P('replica', None, 'tensor')
- mixed_tracker: bfloat16 [16, 2048, 7168], P('replica', None, 'tensor')
The draws below stay inside these ranges and needn't reach their ends.
Inputs may be any that keep to these rules, and one draw needn't show every extreme that they name: `neighbours`: every slot of row r holds r itself or a replica r - o modulo 16 with o one of 1, -1, 2, -2, 4, -4, each o at most once in a row; a row has between 2 and 6 slots that are not r, and some row has 6. `numerators`: A numerator is 0 exactly in slots that hold the row's own replica, and 4 to 8 elsewhere.
All inputs are finite; a program needn't handle non-finite values.
Results may differ from the reference program's by a relative error of at most 0.0058.
Values may be sent and summed in bfloat16 or wider, within the bound.
A program may use at most 128 MiB of HBM per device.

```python
import math
import jax
import jax.numpy as jnp

D = 2048
FF = 7168
TOK = 384
DEG = 6
DEN = 64
REPLICAS = 16


def graph_pattern(key):
    keys = jax.random.split(key, 5)
    row_ids = jnp.arange(REPLICAS, dtype=jnp.int32)
    degrees = jax.random.randint(keys[0], (REPLICAS,), 2, DEG + 1)
    end_rows = (row_ids == 0) | (row_ids == REPLICAS - 1)
    degrees = jnp.where(end_rows, jnp.minimum(degrees, DEG - 1), degrees)
    busiest = jax.random.randint(keys[1], (), 1, REPLICAS - 1)
    sparsest = (busiest + 1 + jax.random.randint(keys[2], (), 0, REPLICAS - 1)) % REPLICAS
    degrees = jnp.where(row_ids == busiest, DEG, jnp.where(row_ids == sparsest, 2, degrees))
    scores = jax.random.randint(keys[3], (REPLICAS, 6), 0, 1 << 20) * 8 + jnp.arange(6, dtype=jnp.int32)[None, :]
    order = jnp.argsort(scores, axis=1)
    table = jnp.array([1, -1, 2, -2, 4, -4], dtype=jnp.int32)
    offsets = table[order][:, :DEG]
    slots = jnp.arange(DEG, dtype=jnp.int32)
    live = slots[None, :] < degrees[:, None]
    linked = jnp.where(live, jnp.mod(row_ids[:, None] - offsets, REPLICAS), row_ids[:, None])
    weights = jnp.where(live, jax.random.randint(keys[4], (REPLICAS, DEG), 4, 9), 0)
    weights = weights.at[busiest, 0].set(8)
    return (linked.astype(jnp.int32), weights.astype(jnp.int32))


def draw_neighbours(key, part):
    linked, weights = graph_pattern(key)
    return linked


def draw_numerators(key, part):
    linked, weights = graph_pattern(key)
    return weights


def level_of(key, shape, pieces, smallest, top_value):
    gain, own = 1.0, jax.random.fold_in(key, 6)
    for axis_at, shards_of in pieces:
        draws = jnp.exp(jax.random.uniform(jax.random.fold_in(own, axis_at), (shards_of,), jnp.float32, smallest / len(pieces), top_value / len(pieces)))
        gain = gain * jnp.repeat(draws, shape[axis_at] // shards_of).reshape([-1 if axis == axis_at else 1 for axis in range(len(shape))])
    return gain


def centred(own_key, dims, width, limit, cuts=(), kind=jnp.bfloat16):
    gain = level_of(own_key, dims, cuts, -0.22, 0.18) if cuts else 1.0
    values = jax.random.normal(own_key, dims, jnp.float32) * width * gain
    return jnp.minimum(jnp.maximum(values, -limit), limit).astype(kind)


def setup_inputs(seed: int = 0) -> dict:
    key_of = jax.random.split(jax.random.key(seed), 10)
    return {
        "tokens": centred(key_of[0], (REPLICAS, TOK, D), 1.0, 6.0, ((0, 16), (1, 16))),
        "targets": centred(key_of[1], (REPLICAS, TOK, D), 1.0, 6.0, ((0, 16), (1, 16))),
        "gate_weight": centred(key_of[2], (REPLICAS, D, FF), 1.0, 6.0, ((0, 16), (2, 16))),
        "probes": centred(key_of[3], (REPLICAS, D, FF), 1.0, 6.0, ((0, 16), (2, 16))),
        "tracker": jnp.clip(jnp.exp(math.log(2.0) - 3.6927934 * jax.random.uniform(key_of[4], (REPLICAS, D, FF), jnp.float32) ** level_of(key_of[4], (REPLICAS, D, FF), ((0, 16), (2, 16)), -0.2, 0.2)), 0.049804688, 2.0).astype(jnp.bfloat16),
        "up_weight": centred(key_of[5], (D, FF), 1.0, 6.0, ((0, 16), (1, 16))),
        "down_weight": centred(key_of[6], (FF, D), 1.0, 6.0, ((0, 16), (1, 16))),
        "neighbours": draw_neighbours(jax.random.fold_in(key_of[9], 71), 0),
        "numerators": draw_numerators(jax.random.fold_in(key_of[9], 71), 0),
    }


step_size = 0.1
floor_value = 0.1
tracker_decay = 0.75

def derivatives(gate_pre):
    logistic = jax.nn.sigmoid(gate_pre)
    activated = gate_pre * logistic
    slope_one = logistic * (1.0 + gate_pre * (1.0 - logistic))
    slope_two = logistic * (1.0 - logistic) * (2.0 + gate_pre * (1.0 - 2.0 * logistic))
    return (activated, slope_one, slope_two)

def replica_pass(tokens_one, targets_one, weight_now, probe, tracker_now, up_weight, down_weight):
    inv_width = 1.0 / math.sqrt(D)
    inv_hidden = 1.0 / math.sqrt(FF)
    gate_pre = jnp.dot(tokens_one, weight_now, preferred_element_type=jnp.float32) * inv_width
    up_pre = jnp.dot(tokens_one, up_weight, preferred_element_type=jnp.float32) * inv_width
    activated, slope_one, slope_two = derivatives(gate_pre)
    hidden = (activated * up_pre).astype(jnp.bfloat16)
    outputs = jnp.dot(hidden, down_weight, preferred_element_type=jnp.float32) * inv_hidden
    residual = (outputs - targets_one.astype(jnp.float32)).astype(jnp.bfloat16)
    grad_hidden = jnp.dot(residual, down_weight.T, preferred_element_type=jnp.float32) * inv_hidden
    grad_gate = (grad_hidden * up_pre * slope_one).astype(jnp.bfloat16)
    gradient = jnp.dot(tokens_one.T, grad_gate, preferred_element_type=jnp.float32) * inv_width
    ratio = gradient / jnp.maximum(tracker_now.astype(jnp.float32), floor_value)
    stepped = (weight_now.astype(jnp.float32) - step_size * jnp.clip(ratio, -1.0, 1.0)).astype(jnp.bfloat16)
    probe_pre = jnp.dot(tokens_one, probe, preferred_element_type=jnp.float32) * inv_width
    tangent_hidden = (slope_one * probe_pre * up_pre).astype(jnp.bfloat16)
    tangent_out = jnp.dot(tangent_hidden, down_weight, preferred_element_type=jnp.float32) * inv_hidden
    tangent_res = tangent_out.astype(jnp.bfloat16)
    tangent_grad = jnp.dot(tangent_res, down_weight.T, preferred_element_type=jnp.float32) * inv_hidden
    tangent_gate = ((tangent_grad * slope_one + grad_hidden * slope_two * probe_pre) * up_pre).astype(jnp.bfloat16)
    curvature_probe = jnp.dot(tokens_one.T, tangent_gate, preferred_element_type=jnp.float32) * inv_width
    tracked = (tracker_decay * tracker_now.astype(jnp.float32) + (1.0 - tracker_decay) * probe.astype(jnp.float32) * curvature_probe).astype(jnp.bfloat16)
    return (stepped, tracked)

def mix_all(stacked, neighbours, numerators):
    mixed_rows = []
    for replica in range(REPLICAS):
        self_weight = (DEN - jnp.sum(numerators[replica])).astype(jnp.float32) / DEN
        mixed_sum = self_weight * stacked[replica].astype(jnp.float32)
        for slot in range(DEG):
            share = numerators[replica, slot].astype(jnp.float32) / DEN
            mixed_sum = mixed_sum + share * stacked[neighbours[replica, slot]].astype(jnp.float32)
        mixed_rows.append(mixed_sum.astype(jnp.bfloat16))
    return jnp.stack(mixed_rows)

def reference(tokens, targets, gate_weight, probes, tracker, up_weight, down_weight, neighbours, numerators):
    stepped_rows = []
    tracked_rows = []
    for replica in range(REPLICAS):
        stepped, tracked = replica_pass(tokens[replica], targets[replica], gate_weight[replica], probes[replica], tracker[replica], up_weight, down_weight)
        stepped_rows.append(stepped)
        tracked_rows.append(tracked)
    mixed_weights = mix_all(jnp.stack(stepped_rows), neighbours, numerators)
    mixed_tracker = mix_all(jnp.stack(tracked_rows), neighbours, numerators)
    return (mixed_weights, mixed_tracker)
```

```python
import functools
import math

import jax
import jax.numpy as jnp
from jax import lax
from jax.experimental import pallas as pl
from jax.experimental.pallas import tpu as pltpu
from jax.sharding import PartitionSpec as P

MESH = pl.DeviceIdType.MESH
D = 2048
FF = 7168
DEN = 64
TOK = 384
COLS = 448
STEP_SIZE = 0.1
FLOOR = 0.1
DECAY = 0.75
INV_WIDTH = 1.0 / math.sqrt(D)
INV_HIDDEN = 1.0 / math.sqrt(FF)

CH = 128
NC = D // CH
PK = CH * 7 // 2
HALF = PK // 2
f32 = jnp.float32
bf16 = jnp.bfloat16


def mod(value, count):
    return lax.rem(value + 4 * count, count)


class Gather:
    def __init__(self, slot, rows, own, sems, zh, x, device):
        self.slot, self.rows, self.own = slot, rows, own
        (self.z_s, self.z_r, self.zf_s, self.zf_r, self.x_s, self.x_r, self.xf_s, self.xf_r) = sems
        self.zh, self.x, self.device = zh, x, device

    def part(self, ref, half):
        size = self.rows // 2
        return ref.at[pl.ds(half * size, size)]

    def z_copy(self, way):
        return pltpu.make_async_remote_copy(
            self.own, self.slot(self.x, self.zh), self.z_s.at[way], self.z_r.at[way],
            device_id=self.device(1 - 2 * way, 0), device_id_type=MESH)

    def z_start(self):
        for way in range(2):
            self.z_copy(way).start()

    def z_forward_copy(self, way):
        block = self.part(self.slot(self.x, mod(self.zh - (1 - 2 * way), 4)), way)
        return pltpu.make_async_remote_copy(
            block, block, self.zf_s.at[way], self.zf_r.at[way],
            device_id=self.device(1 - 2 * way, 0), device_id_type=MESH)

    def z_forward(self):
        for way in range(2):
            self.z_copy(way).wait_recv()
            self.z_forward_copy(way).start()

    def z_last(self):
        for way in range(2):
            self.z_forward_copy(way).wait_recv()

    def x_copy(self, q, way):
        block = self.slot(self.x, mod(self.zh + q, 4))
        return pltpu.make_async_remote_copy(
            self.own if q == 0 else block, block, self.x_s.at[q, way], self.x_r.at[q, way],
            device_id=self.device(0, 1 - 2 * way), device_id_type=MESH)

    def x_start(self, q):
        for way in range(2):
            self.x_copy(q, way).start()

    def x_forward_copy(self, q, way):
        block = self.part(self.slot(mod(self.x - (1 - 2 * way), 4), mod(self.zh + q, 4)), way)
        return pltpu.make_async_remote_copy(
            block, block, self.xf_s.at[q, way], self.xf_r.at[q, way],
            device_id=self.device(0, 1 - 2 * way), device_id_type=MESH)

    def x_forward(self, q):
        for way in range(2):
            self.x_copy(q, way).wait_recv()
            self.x_forward_copy(q, way).start()

    def x_last(self, q):
        for way in range(2):
            self.x_forward_copy(q, way).wait_recv()

    def drain(self):
        for way in range(2):
            self.z_copy(way).wait_send()
            self.z_forward_copy(way).wait_send()
            for q in range(4):
                self.x_copy(q, way).wait_send()
                self.x_forward_copy(q, way).wait_send()


def kernel(
    tok_ref, tgt_ref, w_hbm, p_hbm, h_hbm, up_ref, down_ref, nb_ref, num_ref,
    out_w, out_t,
    w_ref, p_ref, h_ref, tk, pair, x_all, x_turned, upb, dnb,
    gate_acc, probe_acc, up_acc, grad_acc, tang_acc,
    hid, gates, core_send, core_recv, own_part, rs_send, rs_recv, res,
    own_mix, left_mix, right_mix, far_mix, below, above, mine, staged,
    load_sem, tk_s, tk_r, tkf_s, tg_s, tg_r,
    uz_s, uz_r, uzf_s, uzf_r, ux_s, ux_r, uxf_s, uxf_r,
    dz_s, dz_r, dzf_s, dzf_r, dx_s, dx_r, dxf_s, dxf_r,
    cs_s, cs_r, rs_s, rs_r, ag_s, ag_r, ac_s, ac_r,
    mx_s, mx_r, mf_s, mf_r, mz_s, mz_r, out_sem,
):
    r = lax.axis_index("replica")
    t = lax.axis_index("tensor")
    zh, x = r // 4, lax.rem(r, 4)
    chip, core = t // 2, lax.rem(t, 2)
    sibling = (r, 2 * chip + 1 - core)

    def replica_at(dz, dx):
        return mod(zh + dz, 4) * 4 + mod(x + dx, 4)

    def device(dz, dx):
        return (replica_at(dz, dx), t)

    def peer(j):
        return (r, 2 * lax.rem(chip + j, 8) + core)

    def remote(src, dst, send, recv, where):
        return pltpu.make_async_remote_copy(
            src, dst, send, recv, device_id=where, device_id_type=MESH)

    loads = [
        pltpu.make_async_copy(src, dst, load_sem.at[i])
        for i, (src, dst) in enumerate(((w_hbm, w_ref), (p_hbm, p_ref), (h_hbm, h_ref)))
    ]
    for load in loads:
        load.start()

    barrier = pltpu.get_barrier_semaphore()
    partners = [device(1, 0), device(-1, 0), device(0, 1), device(0, -1), sibling]
    for where in partners:
        pl.semaphore_signal(barrier, inc=1, device_id=where, device_id_type=MESH)

    @pl.loop(1, 8)
    def _(j):
        pl.semaphore_signal(barrier, inc=1, device_id=peer(j), device_id_type=MESH)

    def packed_rows(ref):
        block = ref[...].astype(f32)
        return jnp.concatenate([block[:, :1024], block[:, 1024:]], axis=0).astype(bf16)

    tk[t] = packed_rows(tok_ref)
    pair[core] = packed_rows(tgt_ref)
    upb[x, zh] = up_ref[...]
    dnb[x, :, pl.ds(pl.multiple_of(zh * 128, 128), 128)] = down_ref[...]
    pl.semaphore_wait(barrier, 12)

    def tk_copy(j):
        return remote(tk.at[t], tk.at[t], tk_s.at[j], tk_r.at[j], peer(j))

    def tk_from(j):
        slot = 2 * lax.rem(chip + 8 - j, 8) + core
        return remote(tk.at[slot], tk.at[slot], tkf_s.at[j], tk_r.at[j], sibling)

    def tk_pass(j):
        slot = 2 * lax.rem(chip + 8 - j, 8) + core
        return remote(tk.at[slot], tk.at[slot], tkf_s.at[j], tk_r.at[8 + j], sibling)

    target_copy = remote(pair.at[core], pair.at[core], tg_s, tg_r, sibling)

    up_gather = Gather(lambda column, row: upb.at[column, row], 128, up_ref,
                       (uz_s, uz_r, uzf_s, uzf_r, ux_s, ux_r, uxf_s, uxf_r), zh, x, device)
    down_gather = Gather(
        lambda column, row: dnb.at[column, :, pl.ds(pl.multiple_of(row * 128, 128), 128)], COLS, down_ref,
        (dz_s, dz_r, dzf_s, dzf_r, dx_s, dx_r, dxf_s, dxf_r), zh, x, device)

    up_gather.x_start(0)
    up_gather.z_start()

    @pl.loop(1, 8)
    def _(j):
        tk_copy(j).start()

    tk_pass(0).start()
    target_copy.start()
    up_gather.z_forward()
    up_gather.x_start(1)
    up_gather.x_start(3)
    up_gather.x_forward(0)
    down_gather.z_start()
    up_gather.z_last()
    up_gather.x_start(2)

    @pl.loop(1, 8)
    def _(j):
        tk_from(j).wait_recv()
        tk_pass(j).start()

    up_gather.x_forward(1)
    up_gather.x_forward(3)
    down_gather.z_forward()
    down_gather.x_start(0)

    @pl.loop(0, 8)
    def _(j):
        tk_pass(j).wait_recv()

    @pl.loop(0, 8)
    def _(c):
        blocks = [tk[2 * c + k].astype(f32) for k in range(2)]
        rows = [jnp.concatenate([b[:24], b[24:]], axis=1) for b in blocks]
        x_all[pl.ds(pl.multiple_of(c * 48, 48), 48), :] = jnp.concatenate(rows, axis=0).astype(bf16)

    up_gather.x_forward(2)
    down_gather.x_start(1)
    down_gather.x_start(3)

    def wide_dot(acc, weight):
        @pl.loop(0, 4)
        def _(k):
            part = jnp.dot(
                x_all[:, pl.ds(pl.multiple_of(k * 512, 512), 512)],
                weight[pl.ds(pl.multiple_of(k * 512, 512), 512), :],
                preferred_element_type=f32,
            )

            @pl.when(k == 0)
            def _():
                acc[...] = part

            @pl.when(k > 0)
            def _():
                acc[...] += part

    loads[0].wait()
    wide_dot(gate_acc, w_ref)
    down_gather.z_last()
    down_gather.x_start(2)
    loads[1].wait()
    wide_dot(probe_acc, p_ref)
    down_gather.x_forward(0)

    for q in range(4):
        up_gather.x_last(q)

    @pl.loop(0, 4)
    def _(column):
        lanes = [x_all[:, pl.ds(pl.multiple_of(512 * z + 128 * column, 128), 128)] for z in range(4)]
        part = jnp.dot(
            jnp.concatenate(lanes, axis=1), upb[column].reshape(512, COLS), preferred_element_type=f32)

        @pl.when(column == 0)
        def _():
            up_acc[...] = part

        @pl.when(column > 0)
        def _():
            up_acc[...] += part

    @pl.loop(0, 8)
    def _(c):
        rows = pl.ds(pl.multiple_of(c * 48, 48), 48)
        gate_pre = gate_acc[rows, :] * INV_WIDTH
        probe_pre = probe_acc[rows, :] * INV_WIDTH
        up_pre = up_acc[rows, :] * INV_WIDTH
        logistic = jax.nn.sigmoid(gate_pre)
        slope_one = logistic * (1.0 + gate_pre * (1.0 - logistic))
        slope_two = logistic * (1.0 - logistic) * (2.0 + gate_pre * (1.0 - 2.0 * logistic))
        hid[0, rows, :] = (gate_pre * logistic * up_pre).astype(bf16)
        first = up_pre * slope_one
        hid[1, rows, :] = (first * probe_pre).astype(bf16)
        gate_acc[rows, :] = first
        probe_acc[rows, :] = up_pre * slope_two * probe_pre

    down_gather.x_forward(1)
    down_gather.x_forward(3)

    @pl.loop(0, 16)
    def _(c):
        lanes = pl.ds(pl.multiple_of(c * 128, 128), 128)
        x_turned[lanes, :] = x_all[:, lanes].astype(f32).T.astype(bf16)

    target_copy.wait_recv()
    down_gather.x_forward(2)

    columns = [mod(x + step, 4) for step in (0, 3, 1, 2)]

    def lanes_of(k):
        return pl.ds(pl.multiple_of(256 * k, 256), 256)

    def core_copy(s, p):
        return remote(core_send.at[p, s], core_recv.at[p, s], cs_s.at[p, s], cs_r.at[p, s], sibling)

    def forward(s, p):
        away = jnp.dot(hid[p], dnb[columns[s], :, lanes_of(1 - core)], preferred_element_type=f32)
        core_send[p, s] = (away * INV_HIDDEN).astype(bf16)
        core_copy(s, p).start()
        here = jnp.dot(hid[p], dnb[columns[s], :, lanes_of(core)], preferred_element_type=f32)
        own_part[p, s] = here * INV_HIDDEN

    def rs_copy(s, p, j):
        to = lax.rem(chip + j, 8)
        return remote(
            rs_send.at[p, s, pl.ds(pl.multiple_of(48 * to, 48), 48)], rs_recv.at[p, s, j],
            rs_s.at[p, s, j], rs_r.at[p, s, j], peer(j))

    def scatter(s, p):
        core_copy(s, p).wait_recv()
        total = own_part[p, s] + core_recv[p, s].astype(f32)
        own_part[p, s] = total
        rs_send[p, s] = total.astype(bf16)

        @pl.loop(1, 8)
        def _(j):
            rs_copy(s, p, j).start()

    own_rows = pl.ds(pl.multiple_of(48 * chip, 48), 48)

    def ag_copy(s, p, j):
        block = res.at[p, s, core, own_rows]
        return remote(block, block, ag_s.at[p, s, j], ag_r.at[p, s, j], peer(j))

    def reduce(s, p):
        @pl.loop(1, 8)
        def _(j):
            rs_copy(s, p, j).wait_recv()

        total = own_part[p, s, own_rows, :]
        for j in range(1, 8):
            total = total + rs_recv[p, s, j].astype(f32)
        if p == 0:
            target = []
            for k in range(2):
                block = pair[k]
                pieces = []
                for m in range(2):
                    at = pl.ds(pl.multiple_of(512 * m + 128 * columns[s], 128), 128)
                    top = pair[k, :, at].astype(f32)
                    pieces.append(jnp.where(core == 0, top[:24], top[24:]))
                target.append(jnp.concatenate(pieces, axis=1))
            total = total - jnp.concatenate(target, axis=0)
        res[p, s, core, own_rows, :] = total.astype(bf16)

        @pl.loop(1, 8)
        def _(j):
            ag_copy(s, p, j).start()

    def across_copy(s, p, k):
        return remote(res.at[p, s, k], res.at[p, s, k], ac_s.at[p, s], ac_r.at[p, s], sibling)

    def across(s, p):
        @pl.loop(1, 8)
        def _(j):
            ag_copy(s, p, j).wait_recv()

        across_copy(s, p, core).start()

    def backward(s, p, acc):
        across_copy(s, p, 1 - core).wait_recv()
        rows = jnp.concatenate([res[p, s, 0], res[p, s, 1]], axis=1)
        part = lax.dot_general(
            rows, dnb[columns[s]], (((1,), (1,)), ((), ())), preferred_element_type=f32) * INV_HIDDEN
        if s == 0:
            acc[...] = part
        else:
            acc[...] += part

    def ready(s):
        if s == 3:
            for q in range(4):
                down_gather.x_last(q)

    for step in range(8):
        for p in range(2):
            if step < 4:
                if p == 0:
                    ready(step)
                forward(step, p)
            if 0 <= step - 1 < 4:
                scatter(step - 1, p)
            if 0 <= step - 2 < 4:
                reduce(step - 2, p)
            if 0 <= step - 3 < 4:
                across(step - 3, p)
            if 0 <= step - 4 < 4:
                backward(step - 4, p, grad_acc if p == 0 else tang_acc)

    loads[2].wait()

    @pl.loop(0, 8)
    def _(c):
        rows = pl.ds(pl.multiple_of(c * 48, 48), 48)
        grad = grad_acc[rows, :]
        gates[0, rows, :] = (grad * gate_acc[rows, :]).astype(bf16)
        gates[1, rows, :] = (tang_acc[rows, :] * gate_acc[rows, :] + grad * probe_acc[rows, :]).astype(bf16)

    def share(dest, source):
        total = jnp.int32(0)
        for k in range(6):
            total = total + jnp.where(nb_ref[dest, k] == source, num_ref[dest, k], 0)
        return total.astype(f32) * (1.0 / DEN)

    def self_share():
        total = jnp.int32(0)
        for k in range(6):
            total = total + num_ref[r, k]
        return (DEN - total).astype(f32) * (1.0 / DEN)

    sources = [replica_at(0, dx) for dx in (0, -1, 1, 2)]
    here_c = [self_share()] + [share(r, source) for source in sources[1:]]
    up_c = [share(replica_at(1, 0), source) for source in sources]
    down_c = [share(replica_at(-1, 0), source) for source in sources]

    def product(path, rows):
        return jnp.dot(x_turned[rows, :], gates[path], preferred_element_type=f32) * INV_WIDTH

    def put(g, value):
        for b in range(3):
            own_mix[g, pl.ds(b * CH, CH), :] = value[:, 128 * b : 128 * (b + 1)].astype(bf16)
        tail = jnp.concatenate([value[: CH // 2, 384:], value[CH // 2 :, 384:]], axis=1)
        own_mix[g, pl.ds(3 * CH, CH // 2), :] = tail.astype(bf16)

    def produce_step(i):
        rows = pl.ds(pl.multiple_of(i * CH, CH), CH)
        ratio = product(0, rows) / jnp.maximum(h_ref[rows, :].astype(f32), FLOOR)
        put(i, w_ref[rows, :].astype(f32) - STEP_SIZE * jnp.clip(ratio, -1.0, 1.0))

    def produce_track(i):
        rows = pl.ds(pl.multiple_of(i * CH, CH), CH)
        curvature = product(1, rows)
        put(NC + i, DECAY * h_ref[rows, :].astype(f32) + (1.0 - DECAY) * p_ref[rows, :].astype(f32) * curvature)

    def mx_copy(g, way):
        return remote(
            own_mix.at[g], (left_mix if way == 0 else right_mix).at[g],
            mx_s.at[g, way], mx_r.at[g, way], device(0, 1 - 2 * way))

    def mf_copy(g, way):
        part = pl.ds(way * HALF, HALF)
        return remote(
            (left_mix if way == 0 else right_mix).at[g, part], far_mix.at[g, part],
            mf_s.at[g, way], mf_r.at[g, way], device(0, 1 - 2 * way))

    def mz_copy(g, way):
        return remote(
            (left_mix if way == 0 else right_mix).at[g], (below if way == 0 else above).at[g],
            mz_s.at[g, way], mz_r.at[g, way], device(1 - 2 * way, 0))

    def x_send(g):
        for way in range(2):
            mx_copy(g, way).start()

    def x_pass(g):
        for way in range(2):
            mx_copy(g, way).wait_recv()
            mf_copy(g, way).start()

    def z_send(g):
        for way in range(2):
            mf_copy(g, way).wait_recv()
            mf_copy(g, way).wait_send()
        slot = lax.rem(g, 4)

        @pl.loop(0, 4)
        def _(piece):
            rows = pl.ds(pl.multiple_of(piece * (PK // 4), 16), PK // 4)
            parts = [ref[g, rows, :].astype(f32) for ref in (own_mix, left_mix, right_mix, far_mix)]

            def weighted(shares):
                total = shares[0] * parts[0]
                for c, part in zip(shares[1:], parts[1:]):
                    total = total + c * part
                return total

            mine[slot, rows, :] = weighted(here_c)
            left_mix[g, rows, :] = weighted(up_c).astype(bf16)
            right_mix[g, rows, :] = weighted(down_c).astype(bf16)

        for way in range(2):
            mz_copy(g, way).start()

    def out_copy(out, i, slot):
        return pltpu.make_async_copy(
            staged.at[slot], out.at[pl.ds(pl.multiple_of(i * CH, CH), CH)], out_sem.at[slot])

    def finish(out, i, g):
        for way in range(2):
            mz_copy(g, way).wait_recv()
        total = mine[lax.rem(g, 4)] + below[g].astype(f32) + above[g].astype(f32)
        slot = lax.rem(g, 2)

        @pl.when(g >= 2)
        def _():
            out_copy(out, i, slot).wait()

        for b in range(3):
            staged[slot, :, pl.ds(128 * b, 128)] = total[b * CH : (b + 1) * CH].astype(bf16)
        tail = total[3 * CH :]
        last = jnp.concatenate([tail[:, :64], tail[:, 64:]], axis=0)
        staged[slot, :, pl.ds(384, 64)] = last.astype(bf16)
        out_copy(out, i, slot).start()

    produce_step(0)
    x_send(0)
    produce_step(1)
    x_send(1)
    x_pass(0)

    @pl.loop(0, 2 * NC + 2)
    def _(g):
        @pl.when(g + 2 < NC)
        def _():
            produce_step(g + 2)

        @pl.when((g + 2 >= NC) & (g + 2 < 2 * NC))
        def _():
            produce_track(g + 2 - NC)

        @pl.when(g + 2 < 2 * NC)
        def _():
            x_send(g + 2)

        @pl.when(g + 1 < 2 * NC)
        def _():
            x_pass(g + 1)

        @pl.when(g < 2 * NC)
        def _():
            z_send(g)

        @pl.when((g >= 2) & (g < NC + 2))
        def _():
            finish(out_w, g - 2, g - 2)

        @pl.when(g >= NC + 2)
        def _():
            finish(out_t, g - 2 - NC, g - 2)

    for slot in range(2):
        out_copy(out_t, 0, slot).wait()
    up_gather.drain()
    down_gather.drain()
    target_copy.wait_send()

    @pl.loop(0, 8)
    def _(j):
        tk_pass(j).wait_send()

    @pl.loop(1, 8)
    def _(j):
        tk_copy(j).wait_send()
        for s in range(4):
            for p in range(2):
                rs_copy(s, p, j).wait_send()
                ag_copy(s, p, j).wait_send()

    for s in range(4):
        for p in range(2):
            core_copy(s, p).wait_send()
            across_copy(s, p, core).wait_send()

    @pl.loop(0, 2 * NC)
    def _(g):
        for way in range(2):
            mx_copy(g, way).wait_send()
            mz_copy(g, way).wait_send()


def local(
    tokens, targets, gate_weight, probes, tracker, up_weight, down_weight, neighbours, numerators
):
    vmem = pl.BlockSpec(memory_space=pltpu.VMEM)
    hbm = pl.BlockSpec(memory_space=pl.ANY)
    smem = pl.BlockSpec(memory_space=pltpu.SMEM)
    dma = pltpu.SemaphoreType.DMA
    weight = jax.ShapeDtypeStruct((D, COLS), bf16)
    wide = pltpu.VMEM((TOK, COLS), f32)
    mixed = pltpu.VMEM((2 * NC, PK, 128), bf16)
    gather_sems = [dma((2,))] * 4 + [dma((4, 2))] * 4
    mixed_weights, mixed_tracker = pl.pallas_call(
        kernel,
        out_shape=(weight, weight),
        in_specs=[vmem, vmem, hbm, hbm, hbm, vmem, vmem, smem, smem],
        out_specs=(hbm, hbm),
        scratch_shapes=[
            pltpu.VMEM((D, COLS), bf16),
            pltpu.VMEM((D, COLS), bf16),
            pltpu.VMEM((D, COLS), bf16),
            pltpu.VMEM((16, 48, 1024), bf16),
            pltpu.VMEM((2, 48, 1024), bf16),
            pltpu.VMEM((TOK, D), bf16),
            pltpu.VMEM((D, TOK), bf16),
            pltpu.VMEM((4, 4, 128, COLS), bf16),
            pltpu.VMEM((4, COLS, 512), bf16),
            wide, wide, wide, wide, wide,
            pltpu.VMEM((2, TOK, COLS), bf16),
            pltpu.VMEM((2, TOK, COLS), bf16),
            pltpu.VMEM((2, 4, TOK, 256), bf16),
            pltpu.VMEM((2, 4, TOK, 256), bf16),
            pltpu.VMEM((2, 4, TOK, 256), f32),
            pltpu.VMEM((2, 4, TOK, 256), bf16),
            pltpu.VMEM((2, 4, 8, 48, 256), bf16),
            pltpu.VMEM((2, 4, 2, TOK, 256), bf16),
            mixed, mixed, mixed, mixed, mixed, mixed,
            pltpu.VMEM((4, PK, 128), f32),
            pltpu.VMEM((2, CH, COLS), bf16),
            dma((3,)), dma((8,)), dma((16,)), dma((8,)), dma, dma,
            *gather_sems, *gather_sems,
            dma((2, 4)), dma((2, 4)), dma((2, 4, 8)), dma((2, 4, 8)),
            dma((2, 4, 8)), dma((2, 4, 8)), dma((2, 4)), dma((2, 4)),
            dma((2 * NC, 2)), dma((2 * NC, 2)), dma((2 * NC, 2)), dma((2 * NC, 2)),
            dma((2 * NC, 2)), dma((2 * NC, 2)), dma((2,)),
        ],
        compiler_params=pltpu.CompilerParams(
            collective_id=0, has_side_effects=True, vmem_limit_bytes=63 << 20
        ),
        name="step_and_mix",
    )(
        tokens[0], targets[0], gate_weight[0], probes[0], tracker[0], up_weight, down_weight,
        neighbours, numerators,
    )
    return (mixed_weights[None], mixed_tracker[None])


def solution(mesh):
    return jax.shard_map(
        local,
        mesh=mesh,
        in_specs=(
            P("replica", "tensor", None),
            P("replica", "tensor", None),
            P("replica", None, "tensor"),
            P("replica", None, "tensor"),
            P("replica", None, "tensor"),
            P("replica", "tensor"),
            P("tensor", "replica"),
            P(),
            P(),
        ),
        out_specs=(P("replica", None, "tensor"), P("replica", None, "tensor")),
        check_vma=False,
    )
```

```python
import functools
import math

import jax
import jax.numpy as jnp
from jax import lax
from jax.experimental import pallas as pl
from jax.experimental.pallas import tpu as pltpu
from jax.sharding import PartitionSpec as P

MESH = pl.DeviceIdType.MESH
D = 2048
FF = 7168
DEN = 64
TOK = 384
COLS = 448
STEP_SIZE = 0.1
FLOOR = 0.1
DECAY = 0.75
INV_WIDTH = 1.0 / math.sqrt(D)
INV_HIDDEN = 1.0 / math.sqrt(FF)

CH = 128
NC = D // CH
HALF = COLS // 2
f32 = jnp.float32
bf16 = jnp.bfloat16


def mod(value, count):
    return lax.rem(value + 4 * count, count)


class Gather:
    def __init__(self, slot, rows, own, sems, zh, x, device):
        self.slot, self.rows, self.own = slot, rows, own
        (self.z_s, self.z_r, self.zf_s, self.zf_r, self.x_s, self.x_r, self.xf_s, self.xf_r) = sems
        self.zh, self.x, self.device = zh, x, device

    def part(self, ref, half):
        size = self.rows // 2
        return ref.at[pl.ds(half * size, size)]

    def z_copy(self, way):
        return pltpu.make_async_remote_copy(
            self.own, self.slot(self.x, self.zh), self.z_s.at[way], self.z_r.at[way],
            device_id=self.device(1 - 2 * way, 0), device_id_type=MESH)

    def z_start(self):
        for way in range(2):
            self.z_copy(way).start()

    def z_forward_copy(self, way):
        block = self.part(self.slot(self.x, mod(self.zh - (1 - 2 * way), 4)), way)
        return pltpu.make_async_remote_copy(
            block, block, self.zf_s.at[way], self.zf_r.at[way],
            device_id=self.device(1 - 2 * way, 0), device_id_type=MESH)

    def z_forward(self):
        for way in range(2):
            self.z_copy(way).wait_recv()
            self.z_forward_copy(way).start()

    def z_last(self):
        for way in range(2):
            self.z_forward_copy(way).wait_recv()

    def x_copy(self, q, way):
        block = self.slot(self.x, mod(self.zh + q, 4))
        return pltpu.make_async_remote_copy(
            self.own if q == 0 else block, block, self.x_s.at[q, way], self.x_r.at[q, way],
            device_id=self.device(0, 1 - 2 * way), device_id_type=MESH)

    def x_start(self, q):
        for way in range(2):
            self.x_copy(q, way).start()

    def x_forward_copy(self, q, way):
        block = self.part(self.slot(mod(self.x - (1 - 2 * way), 4), mod(self.zh + q, 4)), way)
        return pltpu.make_async_remote_copy(
            block, block, self.xf_s.at[q, way], self.xf_r.at[q, way],
            device_id=self.device(0, 1 - 2 * way), device_id_type=MESH)

    def x_forward(self, q):
        for way in range(2):
            self.x_copy(q, way).wait_recv()
            self.x_forward_copy(q, way).start()

    def x_last(self, q):
        for way in range(2):
            self.x_forward_copy(q, way).wait_recv()

    def drain(self):
        for way in range(2):
            self.z_copy(way).wait_send()
            self.z_forward_copy(way).wait_send()
            for q in range(4):
                self.x_copy(q, way).wait_send()
                self.x_forward_copy(q, way).wait_send()


def kernel(
    tok_ref, tgt_ref, w_hbm, p_hbm, h_hbm, up_ref, down_ref, nb_ref, num_ref,
    out_w, out_t,
    w_ref, p_ref, h_ref, tk, pair, x_all, upb, dnb,
    gate_acc, probe_acc, up_acc, first_turned, second_turned, grad_acc, tang_acc,
    hid, gates, core_send, core_recv, own_part, rs_send, rs_recv, pair_send, pair_recv, res,
    own_mix, left_mix, right_mix, far_mix, below, above, mine, staged,
    load_sem, tk_s, tk_r, tkf_s, tg_s, tg_r,
    uz_s, uz_r, uzf_s, uzf_r, ux_s, ux_r, uxf_s, uxf_r,
    dz_s, dz_r, dzf_s, dzf_r, dx_s, dx_r, dxf_s, dxf_r,
    cs_s, cs_r, rs_s, rs_r, pair_s, pair_r, ag_s, ag_r, ac_s, ac_r,
    mx_s, mx_r, mf_s, mf_r, mz_s, mz_r, out_sem,
):
    r = lax.axis_index("replica")
    t = lax.axis_index("tensor")
    zh, x = r // 4, lax.rem(r, 4)
    chip, core = t // 2, lax.rem(t, 2)
    half, y = chip // 4, lax.rem(chip, 4)
    sibling = (r, 2 * chip + 1 - core)

    def replica_at(dz, dx):
        return mod(zh + dz, 4) * 4 + mod(x + dx, 4)

    def device(dz, dx):
        return (replica_at(dz, dx), t)

    def peer(j):
        return (r, 2 * lax.rem(chip + j, 8) + core)

    def chip_at(a, b):
        return 4 * lax.rem(half + a, 2) + mod(y + b, 4)

    def same_core(a, b):
        return (r, 2 * chip_at(a, b) + core)

    def remote(src, dst, send, recv, where):
        return pltpu.make_async_remote_copy(
            src, dst, send, recv, device_id=where, device_id_type=MESH)

    loads = [
        pltpu.make_async_copy(src, dst, load_sem.at[i])
        for i, (src, dst) in enumerate(((w_hbm, w_ref), (p_hbm, p_ref), (h_hbm, h_ref)))
    ]
    for load in loads:
        load.start()

    barrier = pltpu.get_barrier_semaphore()
    partners = [device(1, 0), device(-1, 0), device(0, 1), device(0, -1), sibling]
    for where in partners:
        pl.semaphore_signal(barrier, inc=1, device_id=where, device_id_type=MESH)

    @pl.loop(1, 8)
    def _(j):
        pl.semaphore_signal(barrier, inc=1, device_id=peer(j), device_id_type=MESH)

    def packed_rows(ref):
        block = ref[...].astype(f32)
        return jnp.concatenate([block[:, :1024], block[:, 1024:]], axis=0).astype(bf16)

    tk[t] = packed_rows(tok_ref)
    pair[core] = packed_rows(tgt_ref)
    upb[x, zh] = up_ref[...]
    dnb[x, zh] = down_ref[...]
    pl.semaphore_wait(barrier, 12)

    def tk_slot(a, b):
        return tk.at[2 * chip_at(a, b) + core]

    def tk_copy(a, b):
        block = tk_slot(a, 0) if b else tk_slot(0, 0)
        where = same_core(0, b) if b else same_core(1, 0)
        return remote(block, block, tk_s.at[4 * a + b], tk_r.at[4 * a + b], where)

    def tk_pass(a, b):
        block = tk_slot(a, -b)
        return remote(block, block, tkf_s.at[4 * a + b], tk_r.at[8 + 4 * a + b], sibling)

    target_copy = remote(pair.at[core], pair.at[core], tg_s, tg_r, sibling)

    def slots(ref):
        return lambda column, row: ref.at[column, row]

    up_gather = Gather(
        slots(upb), COLS, up_ref,
        (uz_s, uz_r, uzf_s, uzf_r, ux_s, ux_r, uxf_s, uxf_r), zh, x, device)
    down_gather = Gather(
        slots(dnb), COLS, down_ref,
        (dz_s, dz_r, dzf_s, dzf_r, dx_s, dx_r, dxf_s, dxf_r), zh, x, device)

    tk_copy(1, 0).start()
    for b in range(1, 4):
        tk_copy(0, b).start()
    up_gather.z_start()
    up_gather.x_start(0)
    tk_pass(0, 0).start()
    target_copy.start()

    tk_copy(1, 0).wait_recv()
    for b in range(1, 4):
        tk_copy(1, b).start()
    tk_pass(1, 0).start()
    up_gather.z_forward()
    up_gather.x_start(1)
    up_gather.x_start(3)
    down_gather.z_start()
    up_gather.x_forward(0)
    for b in range(1, 4):
        tk_copy(0, b).wait_recv()
        tk_pass(0, b).start()
    up_gather.z_last()
    up_gather.x_start(2)
    down_gather.x_start(0)
    up_gather.x_forward(1)
    up_gather.x_forward(3)
    for b in range(1, 4):
        tk_copy(1, b).wait_recv()
        tk_pass(1, b).start()
    down_gather.z_forward()
    down_gather.x_start(1)
    down_gather.x_start(3)
    for a in range(2):
        for b in range(4):
            tk_pass(a, b).wait_recv()

    @pl.loop(0, 8)
    def _(c):
        blocks = [tk[2 * c + k].astype(f32) for k in range(2)]
        rows = [jnp.concatenate([b[:24], b[24:]], axis=1) for b in blocks]
        x_all[pl.ds(pl.multiple_of(c * 48, 48), 48), :] = jnp.concatenate(rows, axis=0).astype(bf16)

    up_gather.x_forward(2)

    def joined(ref, column, first, count):
        return jnp.concatenate([ref[column, first + i] for i in range(count)], axis=1)

    def rows_dot(left, right):
        return lax.dot_general(left, right, (((1,), (1,)), ((), ())), preferred_element_type=f32)

    def wide_dot(acc, weight):
        acc[...] = rows_dot(x_all[...], weight[...])

    loads[0].wait()
    wide_dot(gate_acc, w_ref)
    down_gather.z_last()
    down_gather.x_start(2)
    down_gather.x_forward(0)
    loads[1].wait()
    wide_dot(probe_acc, p_ref)

    for q in range(4):
        up_gather.x_last(q)

    @pl.loop(0, 4)
    def _(column):
        lanes = [x_all[:, pl.ds(pl.multiple_of(512 * z + 128 * column, 128), 128)] for z in range(4)]
        part = rows_dot(jnp.concatenate(lanes, axis=1), joined(upb, column, 0, 4))

        @pl.when(column == 0)
        def _():
            up_acc[...] = part

        @pl.when(column > 0)
        def _():
            up_acc[...] += part

    @pl.loop(0, 8)
    def _(c):
        rows = pl.ds(pl.multiple_of(c * 48, 48), 48)
        gate_pre = gate_acc[rows, :] * INV_WIDTH
        probe_pre = probe_acc[rows, :] * INV_WIDTH
        up_pre = up_acc[rows, :] * INV_WIDTH
        logistic = jax.nn.sigmoid(gate_pre)
        slope_one = logistic * (1.0 + gate_pre * (1.0 - logistic))
        slope_two = logistic * (1.0 - logistic) * (2.0 + gate_pre * (1.0 - 2.0 * logistic))
        hid[0, rows, :] = (gate_pre * logistic * up_pre).astype(bf16)
        first = up_pre * slope_one
        hid[1, rows, :] = (first * probe_pre).astype(bf16)
        gate_acc[rows, :] = first
        probe_acc[rows, :] = up_pre * slope_two * probe_pre

    down_gather.x_forward(1)
    down_gather.x_forward(3)

    target_copy.wait_recv()
    down_gather.x_forward(2)

    columns = [mod(x + step, 4) for step in (0, 3, 1, 2)]

    def column(s, p):
        return columns[s] if p == 0 else lax.rem(x + s, 4)

    def core_copy(s, p):
        return remote(core_send.at[p, s], core_recv.at[p, s], cs_s.at[p, s], cs_r.at[p, s], sibling)

    def forward(s, p):
        away = jnp.dot(hid[p], joined(dnb, column(s, p), 2 * (1 - core), 2), preferred_element_type=f32)
        core_send[p, s] = (away * INV_HIDDEN).astype(bf16)
        core_copy(s, p).start()
        here = jnp.dot(hid[p], joined(dnb, column(s, p), 2 * core, 2), preferred_element_type=f32)
        own_part[p, s] = here * INV_HIDDEN

    def rs_copy(s, p, j):
        to = lax.rem(chip + j, 8)
        return remote(
            rs_send.at[p, s, to // 4, pl.ds(pl.multiple_of(48 * lax.rem(to, 4), 48), 48)], rs_recv.at[p, s, j],
            rs_s.at[p, s, j], rs_r.at[p, s, j], peer(j))

    def core_sum(s, p):
        core_copy(s, p).wait_recv()
        total = own_part[p, s] + core_recv[p, s].astype(f32)
        own_part[p, s] = total
        rs_send[p, s] = total.astype(bf16).reshape(2, TOK // 2, 256)

    def scatter(s, p):
        core_sum(s, p)

        @pl.loop(1, 8)
        def _(j):
            rs_copy(s, p, j).start()

    own_rows = pl.ds(pl.multiple_of(48 * chip, 48), 48)

    def ag_copy(s, p, j):
        block = res.at[p, s, core, own_rows]
        return remote(block, block, ag_s.at[p, s, j], ag_r.at[p, s, j], peer(j))

    def reduce(s, p):
        @pl.loop(1, 8)
        def _(j):
            rs_copy(s, p, j).wait_recv()

        total = own_part[p, s, own_rows, :]
        for j in range(1, 8):
            total = total + rs_recv[p, s, j].astype(f32)
        target = []
        for k in range(2):
            pieces = []
            for m in range(2):
                at = pl.ds(pl.multiple_of(512 * m + 128 * columns[s], 128), 128)
                top = pair[k, :, at].astype(f32)
                pieces.append(jnp.where(core == 0, top[:24], top[24:]))
            target.append(jnp.concatenate(pieces, axis=1))
        total = total - jnp.concatenate(target, axis=0)
        res[p, s, core, own_rows, :] = total.astype(bf16)

        @pl.loop(1, 8)
        def _(j):
            ag_copy(s, p, j).start()

    def across_copy(s, p, k):
        return remote(res.at[p, s, k], res.at[p, s, k], ac_s.at[p, s], ac_r.at[p, s], sibling)

    def across(s, p):
        @pl.loop(1, 8)
        def _(j):
            ag_copy(s, p, j).wait_recv()

        across_copy(s, p, core).start()

    def backward(s, p, acc):
        across_copy(s, p, 1 - core).wait_recv()
        rows = jnp.concatenate([res[p, s, 0], res[p, s, 1]], axis=1)
        part = rows_dot(joined(dnb, column(s, p), 0, 4), rows) * INV_HIDDEN
        if p == 0 and s == 0:
            acc[...] = part
        else:
            acc[...] += part

    def y_copy(s, b):
        rows = pl.ds(pl.multiple_of(48 * mod(y + b, 4), 48), 48)
        return remote(
            rs_send.at[1, s, :, rows], rs_recv.at[1, s, pl.ds(2 * b, 2)],
            rs_s.at[1, s, b], rs_r.at[1, s, b], same_core(0, b))

    def pair_copy(s):
        return remote(pair_send.at[s], pair_recv.at[s], pair_s.at[s], pair_r.at[s], same_core(1, 0))

    def y_scatter(s):
        core_sum(s, 1)
        for b in range(1, 4):
            y_copy(s, b).start()

    def y_reduce(s):
        for b in range(1, 4):
            y_copy(s, b).wait_recv()

        def total(at):
            value = own_part[1, s, pl.ds(pl.multiple_of(48 * (4 * at + y), 48), 48), :]
            for b in range(1, 4):
                value = value + rs_recv[1, s, 2 * b + at].astype(f32)
            return value

        pair_send[s] = total(1 - half).astype(bf16)
        pair_copy(s).start()
        own_part[1, s, own_rows, :] = total(half)

    def t_copy(s, a, b):
        at = chip_at(a, 0) if b else chip
        block = res.at[1, s, core, pl.ds(pl.multiple_of(48 * at, 48), 48)]
        where = same_core(0, b) if b else same_core(1, 0)
        return remote(block, block, ag_s.at[1, s, 4 * a + b], ag_r.at[1, s, 4 * a + b], where)

    def pair_reduce(s):
        pair_copy(s).wait_recv()
        total = own_part[1, s, own_rows, :] + pair_recv[s].astype(f32)
        res[1, s, core, own_rows, :] = total.astype(bf16)
        t_copy(s, 1, 0).start()
        for b in range(1, 4):
            t_copy(s, 0, b).start()

    def pair_pass(s):
        t_copy(s, 1, 0).wait_recv()
        for b in range(1, 4):
            t_copy(s, 1, b).start()

    def t_across(s):
        for a in range(2):
            for b in range(1, 4):
                t_copy(s, a, b).wait_recv()
        across_copy(s, 1, core).start()

    def turn(p):
        source, turned = ((gate_acc, first_turned), (probe_acc, second_turned))[p]

        @pl.loop(0, 3)
        def _(c):
            tokens_at = pl.ds(pl.multiple_of(c * 128, 128), 128)
            turned[:, tokens_at] = source[tokens_at, :].T

    def ready(s):
        if s == 3:
            for q in range(4):
                down_gather.x_last(q)

    for step in range(8):
        if step < 4:
            ready(step)
            forward(step, 0)
        if 0 <= step - 1 < 4:
            scatter(step - 1, 0)
        if step in (4, 5):
            turn(step - 4)
        if 0 <= step - 2 < 4:
            reduce(step - 2, 0)
        if 0 <= step - 3 < 4:
            across(step - 3, 0)
        if 0 <= step - 4 < 4:
            backward(step - 4, 0, grad_acc)

    loads[2].wait()
    tang_acc[...] = jnp.zeros_like(tang_acc)

    @pl.loop(0, 7)
    def _(c):
        rows = pl.ds(pl.multiple_of(c * 64, 64), 64)
        gates[0, rows, :] = (grad_acc[rows, :] * first_turned[rows, :]).astype(bf16)

    def tangent_gates():
        @pl.loop(0, 7)
        def _(c):
            rows = pl.ds(pl.multiple_of(c * 64, 64), 64)
            gates[1, rows, :] = (
                tang_acc[rows, :] * first_turned[rows, :] + grad_acc[rows, :] * second_turned[rows, :]
            ).astype(bf16)

    tangent_steps = (
        lambda s: forward(s, 1),
        y_scatter,
        y_reduce,
        pair_reduce,
        pair_pass,
        t_across,
        lambda s: backward(s, 1, tang_acc),
    )

    def share(dest, source):
        total = jnp.int32(0)
        for k in range(6):
            total = total + jnp.where(nb_ref[k, dest] == source, num_ref[k, dest], 0)
        return total.astype(f32) * (1.0 / DEN)

    def self_share():
        total = jnp.int32(0)
        for k in range(6):
            total = total + num_ref[k, r]
        return (DEN - total).astype(f32) * (1.0 / DEN)

    sources = [replica_at(0, dx) for dx in (0, -1, 1, 2)]
    here_c = [self_share()] + [share(r, source) for source in sources[1:]]
    up_c = [share(replica_at(1, 0), source) for source in sources]
    down_c = [share(replica_at(-1, 0), source) for source in sources]

    def produce(path, pair_at):
        lanes = pl.ds(pl.multiple_of(pair_at * 256, 256), 256)
        change = jnp.dot(gates[path], x_all[:, lanes], preferred_element_type=f32) * INV_WIDTH
        old = h_ref[:, lanes].astype(f32)
        if path == 0:
            ratio = change / jnp.maximum(old, FLOOR)
            new = w_ref[:, lanes].astype(f32) - STEP_SIZE * jnp.clip(ratio, -1.0, 1.0)
        else:
            new = DECAY * old + (1.0 - DECAY) * p_ref[:, lanes].astype(f32) * change
        for m in range(2):
            own_mix[path * NC + 2 * pair_at + m] = new[:, 128 * m : 128 * (m + 1)].astype(bf16)

    def mx_copy(g, way):
        return remote(
            own_mix.at[g], (left_mix if way == 0 else right_mix).at[g],
            mx_s.at[g, way], mx_r.at[g, way], device(0, 1 - 2 * way))

    def mf_copy(g, way):
        part = pl.ds(way * HALF, HALF)
        return remote(
            (left_mix if way == 0 else right_mix).at[g, part], far_mix.at[g, part],
            mf_s.at[g, way], mf_r.at[g, way], device(0, 1 - 2 * way))

    def mz_copy(g, way):
        return remote(
            (left_mix if way == 0 else right_mix).at[g], (below if way == 0 else above).at[g],
            mz_s.at[g, way], mz_r.at[g, way], device(1 - 2 * way, 0))

    def x_send(g):
        for way in range(2):
            mx_copy(g, way).start()

    def x_pass(g):
        for way in range(2):
            mx_copy(g, way).wait_recv()
            mf_copy(g, way).start()

    def z_send(g):
        for way in range(2):
            mf_copy(g, way).wait_recv()
            mf_copy(g, way).wait_send()
        slot = lax.rem(g, 4)

        @pl.loop(0, 4)
        def _(piece):
            rows = pl.ds(pl.multiple_of(piece * (COLS // 4), 16), COLS // 4)
            parts = [ref[g, rows, :].astype(f32) for ref in (own_mix, left_mix, right_mix, far_mix)]

            def weighted(shares):
                total = shares[0] * parts[0]
                for c, part in zip(shares[1:], parts[1:]):
                    total = total + c * part
                return total

            mine[slot, rows, :] = weighted(here_c)
            left_mix[g, rows, :] = weighted(up_c).astype(bf16)
            right_mix[g, rows, :] = weighted(down_c).astype(bf16)

        for way in range(2):
            mz_copy(g, way).start()

    def out_copy(out, i, slot):
        return pltpu.make_async_copy(
            staged.at[slot], out.at[:, pl.ds(pl.multiple_of(i * CH, CH), CH)], out_sem.at[slot])

    def finish(out, i, g):
        for way in range(2):
            mz_copy(g, way).wait_recv()
        total = mine[lax.rem(g, 4)] + below[g].astype(f32) + above[g].astype(f32)
        slot = lax.rem(g, 2)

        @pl.when(g >= 2)
        def _():
            out_copy(out, i, slot).wait()

        staged[slot] = total.astype(bf16)
        out_copy(out, i, slot).start()

    produce(0, 0)
    x_send(0)
    x_send(1)
    produce(0, 1)
    x_pass(0)

    @pl.loop(0, 2 * NC + 2)
    def _(g):
        ahead = (g + 4) // 2

        @pl.when((lax.rem(g, 2) == 0) & (ahead < NC // 2))
        def _():
            produce(0, ahead)

        @pl.when((lax.rem(g, 2) == 0) & (ahead >= NC // 2) & (ahead < NC))
        def _():
            produce(1, ahead - NC // 2)

        @pl.when(g + 2 < 2 * NC)
        def _():
            x_send(g + 2)

        @pl.when(g + 1 < 2 * NC)
        def _():
            x_pass(g + 1)

        @pl.when(g < 2 * NC)
        def _():
            z_send(g)

        for lag, tangent_step in enumerate(tangent_steps):
            @pl.when((g >= lag) & (g < lag + 4))
            def _(lag=lag, tangent_step=tangent_step):
                tangent_step(g - lag)

        @pl.when(g == len(tangent_steps) + 3)
        def _():
            tangent_gates()

        @pl.when((g >= 2) & (g < NC + 2))
        def _():
            finish(out_w, g - 2, g - 2)

        @pl.when(g >= NC + 2)
        def _():
            finish(out_t, g - 2 - NC, g - 2)

    for slot in range(2):
        out_copy(out_t, 0, slot).wait()
    up_gather.drain()
    down_gather.drain()
    target_copy.wait_send()

    for a in range(2):
        for b in range(4):
            tk_pass(a, b).wait_send()
            if a or b:
                tk_copy(a, b).wait_send()

    @pl.loop(1, 8)
    def _(j):
        for s in range(4):
            rs_copy(s, 0, j).wait_send()
            ag_copy(s, 0, j).wait_send()

    @pl.loop(0, 4)
    def _(s):
        pair_copy(s).wait_send()
        t_copy(s, 1, 0).wait_send()
        for b in range(1, 4):
            y_copy(s, b).wait_send()
            for a in range(2):
                t_copy(s, a, b).wait_send()

    for s in range(4):
        for p in range(2):
            core_copy(s, p).wait_send()
            across_copy(s, p, core).wait_send()

    @pl.loop(0, 2 * NC)
    def _(g):
        for way in range(2):
            mx_copy(g, way).wait_send()
            mz_copy(g, way).wait_send()


def local(
    tokens, targets, gate_weight, probes, tracker, up_weight, down_weight, neighbours, numerators
):
    vmem = pl.BlockSpec(memory_space=pltpu.VMEM)
    hbm = pl.BlockSpec(memory_space=pl.ANY)
    smem = pl.BlockSpec(memory_space=pltpu.SMEM)
    dma = pltpu.SemaphoreType.DMA
    weight = jax.ShapeDtypeStruct((COLS, D), bf16)
    wide = pltpu.VMEM((TOK, COLS), f32)
    turned = pltpu.VMEM((COLS, TOK), f32)
    mixed = pltpu.VMEM((2 * NC, COLS, CH), bf16)
    gather_sems = [dma((2,))] * 4 + [dma((4, 2))] * 4
    mixed_weights, mixed_tracker = pl.pallas_call(
        kernel,
        out_shape=(weight, weight),
        in_specs=[vmem, vmem, hbm, hbm, hbm, vmem, vmem, smem, smem],
        out_specs=(hbm, hbm),
        scratch_shapes=[
            pltpu.VMEM((COLS, D), bf16),
            pltpu.VMEM((COLS, D), bf16),
            pltpu.VMEM((COLS, D), bf16),
            pltpu.VMEM((16, 48, 1024), bf16),
            pltpu.VMEM((2, 48, 1024), bf16),
            pltpu.VMEM((TOK, D), bf16),
            pltpu.VMEM((4, 4, COLS, 128), bf16),
            pltpu.VMEM((4, 4, COLS, 128), bf16),
            wide, wide, wide, turned, turned, turned, turned,
            pltpu.VMEM((2, TOK, COLS), bf16),
            pltpu.VMEM((2, COLS, TOK), bf16),
            pltpu.VMEM((2, 4, TOK, 256), bf16),
            pltpu.VMEM((2, 4, TOK, 256), bf16),
            pltpu.VMEM((2, 4, TOK, 256), f32),
            pltpu.VMEM((2, 4, 2, TOK // 2, 256), bf16),
            pltpu.VMEM((2, 4, 8, 48, 256), bf16),
            pltpu.VMEM((4, 48, 256), bf16),
            pltpu.VMEM((4, 48, 256), bf16),
            pltpu.VMEM((2, 4, 2, TOK, 256), bf16),
            mixed, mixed, mixed, mixed, mixed, mixed,
            pltpu.VMEM((4, COLS, CH), f32),
            pltpu.VMEM((2, COLS, CH), bf16),
            dma((3,)), dma((8,)), dma((16,)), dma((8,)), dma, dma,
            *gather_sems, *gather_sems,
            dma((2, 4)), dma((2, 4)), dma((2, 4, 8)), dma((2, 4, 8)), dma((4,)), dma((4,)),
            dma((2, 4, 8)), dma((2, 4, 8)), dma((2, 4)), dma((2, 4)),
            dma((2 * NC, 2)), dma((2 * NC, 2)), dma((2 * NC, 2)), dma((2 * NC, 2)),
            dma((2 * NC, 2)), dma((2 * NC, 2)), dma((2,)),
        ],
        compiler_params=pltpu.CompilerParams(
            collective_id=0, has_side_effects=True, vmem_limit_bytes=63 << 20
        ),
        name="step_and_mix",
    )(
        tokens[0], targets[0], gate_weight[0].T, probes[0].T, tracker[0].T, up_weight.T, down_weight,
        neighbours.T, numerators.T,
    )
    return (mixed_weights.T[None], mixed_tracker.T[None])


def solution(mesh):
    return jax.shard_map(
        local,
        mesh=mesh,
        in_specs=(
            P("replica", "tensor", None),
            P("replica", "tensor", None),
            P("replica", None, "tensor"),
            P("replica", None, "tensor"),
            P("replica", None, "tensor"),
            P("replica", "tensor"),
            P("tensor", "replica"),
            P(),
            P(),
        ),
        out_specs=(P("replica", None, "tensor"), P("replica", None, "tensor")),
        check_vma=False,
    )
```

```python
import functools
import math

import jax
import jax.numpy as jnp
from jax import lax
from jax.experimental import pallas as pl
from jax.experimental.pallas import tpu as pltpu
from jax.sharding import PartitionSpec as P

MESH = pl.DeviceIdType.MESH
D = 2048
FF = 7168
DEN = 64
TOK = 384
COLS = 448
STEP_SIZE = 0.1
FLOOR = 0.1
DECAY = 0.75
INV_WIDTH = 1.0 / math.sqrt(D)
INV_HIDDEN = 1.0 / math.sqrt(FF)

CH = 128
NC = D // CH
HALF = COLS // 2
RING = 8
f32 = jnp.float32
bf16 = jnp.bfloat16


def mod(value, count):
    return lax.rem(value + 4 * count, count)


class Gather:
    def __init__(self, ref, rows, own, sems, zh, x, device):
        self.ref, self.slot, self.rows, self.own = ref, lambda column, row: ref.at[row, column], rows, own
        (self.sent, self.z_r, self.zf_r, self.x_r, self.xf_r) = sems
        self.zh, self.x, self.device = zh, x, device

    def part(self, ref, half):
        size = self.rows // 2
        return ref.at[pl.ds(half * size, size)]

    def z_copy(self, way):
        return pltpu.make_async_remote_copy(
            self.own, self.slot(self.x, self.zh), self.sent.at[0], self.z_r.at[way],
            device_id=self.device(1 - 2 * way, 0), device_id_type=MESH)

    def z_start(self):
        for way in range(2):
            self.z_copy(way).start()

    def z_forward_copy(self, way):
        block = self.part(self.slot(self.x, mod(self.zh - (1 - 2 * way), 4)), way)
        return pltpu.make_async_remote_copy(
            block, block, self.sent.at[0], self.zf_r,
            device_id=self.device(1 - 2 * way, 0), device_id_type=MESH)

    def z_forward(self):
        for way in range(2):
            self.z_copy(way).wait_recv()
            self.z_forward_copy(way).start()

    def whole(self, block, send, recv):
        return pltpu.make_async_remote_copy(
            block, block, send, recv, device_id=self.device(1, 0), device_id_type=MESH)

    def z_last(self):
        self.whole(self.slot(self.x, mod(self.zh + 2, 4)), self.sent.at[0], self.zf_r).wait_recv()

    def x_copy(self, q, way):
        block = self.slot(self.x, mod(self.zh + q, 4))
        return pltpu.make_async_remote_copy(
            self.own if q == 0 else block, block, self.sent.at[1], self.x_r.at[q, way],
            device_id=self.device(0, 1 - 2 * way), device_id_type=MESH)

    def x_start(self, q):
        for way in range(2):
            self.x_copy(q, way).start()

    def x_forward_copy(self, q, way):
        block = self.part(self.slot(mod(self.x - (1 - 2 * way), 4), mod(self.zh + q, 4)), way)
        return pltpu.make_async_remote_copy(
            block, block, self.sent.at[2], self.xf_r.at[q],
            device_id=self.device(0, 1 - 2 * way), device_id_type=MESH)

    def x_forward(self, q):
        for way in range(2):
            self.x_copy(q, way).wait_recv()
            self.x_forward_copy(q, way).start()

    def x_last(self, q):
        block = self.slot(mod(self.x + 2, 4), mod(self.zh + q, 4))
        self.whole(block, self.sent.at[2], self.xf_r.at[q]).wait_recv()

    def drain(self):
        for i, blocks in enumerate((self.ref.at[0, pl.ds(0, 3)], self.ref.at[pl.ds(0, 2)], self.ref.at[0])):
            self.whole(blocks, self.sent.at[i], self.zf_r).wait_send()


def kernel(
    tok_ref, tgt_ref, w_hbm, p_hbm, h_hbm, up_ref, down_ref, nb_hbm, num_hbm,
    out_w, out_t,
    nb_ref, num_ref,
    w_ref, p_ref, h_ref, tk, pair, x_all, upb, dnb,
    gate_acc, probe_acc, up_acc, first_turned, second_turned, grad_acc, tang_acc,
    hid, gates, core_send, core_recv, own_part, rs_send, rs_recv, pair_send, pair_recv, res,
    own_mix, left_mix, right_mix, far_mix, below, above, mine, staged,
    load_sem, tk_s, tk_r, tg_s, tg_r,
    u_s, uz_r, uzf_r, ux_r, uxf_r,
    d_s, dz_r, dzf_r, dx_r, dxf_r,
    cs_s, cs_r, rs_s, rs_r, pair_s, pair_r, ag_s, ag_r, agp_r, ac_s, ac_r,
    mx_s, mx_r, mf_s, mf_r, mz_s, mz_r, out_sem,
):
    r = lax.axis_index("replica")
    t = lax.axis_index("tensor")
    zh, x = r // 4, lax.rem(r, 4)
    chip, core = t // 2, lax.rem(t, 2)
    half, y = chip // 4, lax.rem(chip, 4)
    sibling = (r, 2 * chip + 1 - core)

    def replica_at(dz, dx):
        return mod(zh + dz, 4) * 4 + mod(x + dx, 4)

    def device(dz, dx):
        return (replica_at(dz, dx), t)

    def peer(j):
        return (r, 2 * lax.rem(chip + j, 8) + core)

    def chip_at(a, b):
        return 4 * lax.rem(half + a, 2) + mod(y + b, 4)

    def same_core(a, b):
        return (r, 2 * chip_at(a, b) + core)

    def remote(src, dst, send, recv, where):
        return pltpu.make_async_remote_copy(
            src, dst, send, recv, device_id=where, device_id_type=MESH)

    barrier = pltpu.get_barrier_semaphore()
    partners = [device(1, 0), device(-1, 0), device(0, 1), device(0, -1), sibling]
    for where in partners:
        pl.semaphore_signal(barrier, inc=1, device_id=where, device_id_type=MESH)

    @pl.loop(1, 8)
    def _(j):
        pl.semaphore_signal(barrier, inc=1, device_id=peer(j), device_id_type=MESH)

    locals_in = (
        (up_ref, upb.at[zh, x]), (down_ref, dnb.at[zh, x]), (w_hbm, w_ref), (p_hbm, p_ref),
        (h_hbm, h_ref), (nb_hbm, nb_ref), (num_hbm, num_ref),
    )
    loads = [
        pltpu.make_async_copy(src, dst, load_sem.at[i]) for i, (src, dst) in enumerate(locals_in)
    ]
    for load in loads:
        load.start()

    def packed_rows(ref):
        block = ref[...].astype(f32)
        return jnp.concatenate([block[:, :1024], block[:, 1024:]], axis=0).astype(bf16)

    tk[t] = packed_rows(tok_ref)
    pair[core] = packed_rows(tgt_ref)
    pl.semaphore_wait(barrier, 12)

    def tk_slot(a, b):
        return tk.at[2 * chip_at(a, b) + core]

    def tk_copy(a, b):
        block = tk_slot(a, 0) if b else tk_slot(0, 0)
        where = same_core(0, b) if b else same_core(1, 0)
        return remote(block, block, tk_s.at[0], tk_r.at[2 * a + (b > 0)], where)

    def tk_pass(a, b):
        block = tk_slot(a, -b)
        return remote(block, block, tk_s.at[1], tk_r.at[0], sibling)

    def tk_wait(count, send, recv):
        return remote(tk.at[pl.ds(0, count)], tk.at[pl.ds(0, count)], tk_s.at[send], tk_r.at[recv], sibling)

    target_copy = remote(pair.at[core], pair.at[core], tg_s, tg_r, sibling)

    up_gather = Gather(upb, COLS, up_ref, (u_s, uz_r, uzf_r, ux_r, uxf_r), zh, x, device)
    down_gather = Gather(dnb, COLS, down_ref, (d_s, dz_r, dzf_r, dx_r, dxf_r), zh, x, device)

    tk_copy(1, 0).start()
    for b in range(1, 4):
        tk_copy(0, b).start()
    up_gather.z_start()
    up_gather.x_start(0)
    tk_pass(0, 0).start()
    target_copy.start()

    tk_copy(1, 0).wait_recv()
    for b in range(1, 4):
        tk_copy(1, b).start()
    tk_pass(1, 0).start()
    down_gather.x_start(0)
    up_gather.x_forward(0)
    up_gather.z_forward()
    up_gather.x_start(1)
    up_gather.x_start(3)
    down_gather.z_start()
    tk_wait(3, 0, 1).wait_recv()
    for b in range(1, 4):
        tk_pass(0, b).start()
    down_gather.x_forward(0)
    up_gather.z_last()
    up_gather.x_start(2)
    tk_wait(3, 0, 3).wait_recv()
    for b in range(1, 4):
        tk_pass(1, b).start()
    up_gather.x_forward(1)
    tk_wait(8, 1, 0).wait_recv()

    @pl.loop(0, 8)
    def _(c):
        blocks = [tk[2 * c + k].astype(f32) for k in range(2)]
        rows = [jnp.concatenate([b[:24], b[24:]], axis=1) for b in blocks]
        x_all[pl.ds(pl.multiple_of(c * 48, 48), 48), :] = jnp.concatenate(rows, axis=0).astype(bf16)

    up_gather.x_forward(3)
    down_gather.z_forward()
    down_gather.x_start(1)
    down_gather.x_start(3)

    def joined(ref, row, first, count):
        return jnp.concatenate([ref[row, first + i] for i in range(count)], axis=1)

    def rows_dot(left, right):
        return lax.dot_general(left, right, (((1,), (1,)), ((), ())), preferred_element_type=f32)

    def wide_dot(acc, weight):
        acc[...] = rows_dot(x_all[...], weight[...])

    loads[2].wait()
    wide_dot(gate_acc, w_ref)
    up_gather.x_forward(2)
    loads[3].wait()
    wide_dot(probe_acc, p_ref)
    down_gather.z_last()
    down_gather.x_start(2)
    loads[0].wait()
    loads[1].wait()

    def up_rows(q):
        row = mod(zh + q, 4)
        return rows_dot(x_all[:, pl.ds(pl.multiple_of(512 * row, 512), 512)], joined(upb, row, 0, 4))

    for q in (0, 1, 3):
        up_gather.x_last(q)
    up_acc[...] = up_rows(0) + up_rows(1) + up_rows(3)
    up_gather.x_last(2)
    up_acc[...] += up_rows(2)

    @pl.loop(0, 8)
    def _(c):
        rows = pl.ds(pl.multiple_of(c * 48, 48), 48)
        gate_pre = gate_acc[rows, :] * INV_WIDTH
        probe_pre = probe_acc[rows, :] * INV_WIDTH
        up_pre = up_acc[rows, :] * INV_WIDTH
        logistic = jax.nn.sigmoid(gate_pre)
        slope_one = logistic * (1.0 + gate_pre * (1.0 - logistic))
        slope_two = logistic * (1.0 - logistic) * (2.0 + gate_pre * (1.0 - 2.0 * logistic))
        hid[0, rows, :] = (gate_pre * logistic * up_pre).astype(bf16)
        first = up_pre * slope_one
        hid[1, rows, :] = (first * probe_pre).astype(bf16)
        gate_acc[rows, :] = first
        probe_acc[rows, :] = up_pre * slope_two * probe_pre

    target_copy.wait_recv()

    order = (0, 1, 3, 2)

    def column(s, p):
        return mod(zh + order[s], 4) if p == 0 else lax.rem(zh + s, 4)

    def core_copy(s, p):
        return remote(core_send.at[p, s], core_recv.at[p, s], cs_s, cs_r.at[p, s], sibling)

    def forward(s, p):
        away = jnp.dot(hid[p], joined(dnb, column(s, p), 2 * (1 - core), 2), preferred_element_type=f32)
        core_send[p, s] = (away * INV_HIDDEN).astype(bf16)
        core_copy(s, p).start()
        here = jnp.dot(hid[p], joined(dnb, column(s, p), 2 * core, 2), preferred_element_type=f32)
        own_part[p, s] = here * INV_HIDDEN

    def blocks_wait(blocks, send, recv):
        return remote(blocks, blocks, send, recv, sibling)

    def rs_copy(s, p, j):
        to = lax.rem(chip + j, 8)
        return remote(
            rs_send.at[p, s, to // 4, pl.ds(pl.multiple_of(48 * lax.rem(to, 4), 48), 48)], rs_recv.at[p, s, j],
            rs_s.at[p], rs_r.at[p, s], peer(j))

    def core_sum(s, p):
        core_copy(s, p).wait_recv()
        total = own_part[p, s] + core_recv[p, s].astype(f32)
        own_part[p, s] = total
        rs_send[p, s] = total.astype(bf16).reshape(2, TOK // 2, 256)

    def scatter(s, p):
        core_sum(s, p)

        @pl.loop(1, 8)
        def _(j):
            rs_copy(s, p, j).start()

    own_rows = pl.ds(pl.multiple_of(48 * chip, 48), 48)

    def ag_copy(s, p, j):
        block = res.at[p, s, core, own_rows]
        return remote(block, block, ag_s.at[p], ag_r.at[p, s], peer(j))

    def reduce(s, p):
        blocks_wait(rs_recv.at[p, s, pl.ds(1, 7)], rs_s.at[p], rs_r.at[p, s]).wait_recv()
        total = own_part[p, s, own_rows, :]
        for j in range(1, 8):
            total = total + rs_recv[p, s, j].astype(f32)
        row = column(s, p)
        at = pl.ds(pl.multiple_of(512 * lax.rem(row, 2) + 256 * core, 256), 256)
        target = []
        for k in range(2):
            both = pair[k, :, at].astype(f32)
            target.append(jnp.where(row < 2, both[:24], both[24:]))
        total = total - jnp.concatenate(target, axis=0)
        res[p, s, core, own_rows, :] = total.astype(bf16)

        @pl.loop(1, 8)
        def _(j):
            ag_copy(s, p, j).start()

    def across_copy(s, p, k):
        return remote(res.at[p, s, k], res.at[p, s, k], ac_s, ac_r.at[p, s], sibling)

    def across(s, p):
        blocks_wait(rs_recv.at[p, s, pl.ds(1, 7)], ag_s.at[p], ag_r.at[p, s]).wait_recv()
        across_copy(s, p, core).start()

    def backward(s, p, acc):
        across_copy(s, p, 1 - core).wait_recv()
        rows = jnp.concatenate([res[p, s, 0], res[p, s, 1]], axis=1)
        part = rows_dot(joined(dnb, column(s, p), 0, 4), rows) * INV_HIDDEN
        if p == 0 and s == 0:
            acc[...] = part
        else:
            acc[...] += part

    def y_copy(s, b):
        rows = pl.ds(pl.multiple_of(48 * mod(y + b, 4), 48), 48)
        return remote(
            rs_send.at[1, s, :, rows], rs_recv.at[1, s, pl.ds(2 * b, 2)],
            rs_s.at[1], rs_r.at[1, s], same_core(0, b))

    def pair_copy(s):
        return remote(pair_send.at[s], pair_recv.at[s], pair_s, pair_r.at[s], same_core(1, 0))

    def y_scatter(s):
        core_sum(s, 1)
        for b in range(1, 4):
            y_copy(s, b).start()

    def y_reduce(s):
        blocks_wait(rs_recv.at[1, s, pl.ds(2, 6)], rs_s.at[1], rs_r.at[1, s]).wait_recv()

        def total(at):
            value = own_part[1, s, pl.ds(pl.multiple_of(48 * (4 * at + y), 48), 48), :]
            for b in range(1, 4):
                value = value + rs_recv[1, s, 2 * b + at].astype(f32)
            return value

        pair_send[s] = total(1 - half).astype(bf16)
        pair_copy(s).start()
        own_part[1, s, own_rows, :] = total(half)

    def t_copy(s, a, b):
        at = chip_at(a, 0) if b else chip
        block = res.at[1, s, core, pl.ds(pl.multiple_of(48 * at, 48), 48)]
        where = same_core(0, b) if b else same_core(1, 0)
        return remote(block, block, ag_s.at[1], ag_r.at[1, s] if b else agp_r.at[s], where)

    def pair_reduce(s):
        pair_copy(s).wait_recv()
        total = own_part[1, s, own_rows, :] + pair_recv[s].astype(f32)
        res[1, s, core, own_rows, :] = total.astype(bf16)
        t_copy(s, 1, 0).start()
        for b in range(1, 4):
            t_copy(s, 0, b).start()

    def pair_pass(s):
        t_copy(s, 1, 0).wait_recv()
        for b in range(1, 4):
            t_copy(s, 1, b).start()

    def t_across(s):
        blocks_wait(rs_recv.at[1, s, pl.ds(2, 6)], ag_s.at[1], ag_r.at[1, s]).wait_recv()
        across_copy(s, 1, core).start()

    def turn(p):
        source, turned = ((gate_acc, first_turned), (probe_acc, second_turned))[p]

        @pl.loop(0, 3)
        def _(c):
            tokens_at = pl.ds(pl.multiple_of(c * 128, 128), 128)
            turned[:, tokens_at] = source[tokens_at, :].T

    def ready(s):
        down_gather.x_last(order[s])

    def passed_on(step):
        if step < 3:
            down_gather.x_forward(order[step + 1])

    for step in range(8):
        if step < 4:
            ready(step)
            forward(step, 0)
            passed_on(step)
        if 0 <= step - 1 < 4:
            scatter(step - 1, 0)
        if step in (4, 5):
            turn(step - 4)
        if 0 <= step - 2 < 4:
            reduce(step - 2, 0)
        if 0 <= step - 3 < 4:
            across(step - 3, 0)
        if 0 <= step - 4 < 4:
            backward(step - 4, 0, grad_acc)

    loads[4].wait()
    tang_acc[...] = jnp.zeros_like(tang_acc)

    @pl.loop(0, 7)
    def _(c):
        rows = pl.ds(pl.multiple_of(c * 64, 64), 64)
        gates[0, rows, :] = (grad_acc[rows, :] * first_turned[rows, :]).astype(bf16)

    def tangent_gates():
        @pl.loop(0, 7)
        def _(c):
            rows = pl.ds(pl.multiple_of(c * 64, 64), 64)
            gates[1, rows, :] = (
                tang_acc[rows, :] * first_turned[rows, :] + grad_acc[rows, :] * second_turned[rows, :]
            ).astype(bf16)

    tangent_steps = (
        lambda s: forward(s, 1),
        y_scatter,
        y_reduce,
        pair_reduce,
        pair_pass,
        t_across,
        lambda s: backward(s, 1, tang_acc),
    )

    def share(dest, source):
        total = jnp.int32(0)
        for k in range(6):
            total = total + jnp.where(nb_ref[k, dest] == source, num_ref[k, dest], 0)
        return total.astype(f32) * (1.0 / DEN)

    def self_share():
        total = jnp.int32(0)
        for k in range(6):
            total = total + num_ref[k, r]
        return (DEN - total).astype(f32) * (1.0 / DEN)

    loads[5].wait()
    loads[6].wait()
    sources = [replica_at(0, dx) for dx in (0, -1, 1, 2)]
    here_c = [self_share()] + [share(r, source) for source in sources[1:]]
    up_c = [share(replica_at(1, 0), source) for source in sources]
    down_c = [share(replica_at(-1, 0), source) for source in sources]

    def produce(path, pair_at):
        lanes = pl.ds(pl.multiple_of(pair_at * 256, 256), 256)
        change = jnp.dot(gates[path], x_all[:, lanes], preferred_element_type=f32) * INV_WIDTH
        old = h_ref[:, lanes].astype(f32)
        if path == 0:
            ratio = change / jnp.maximum(old, FLOOR)
            new = w_ref[:, lanes].astype(f32) - STEP_SIZE * jnp.clip(ratio, -1.0, 1.0)
        else:
            new = DECAY * old + (1.0 - DECAY) * p_ref[:, lanes].astype(f32) * change
        for m in range(2):
            own_mix[path * NC + 2 * pair_at + m] = new[:, 128 * m : 128 * (m + 1)].astype(bf16)

    def mx_copy(g, way):
        return remote(
            own_mix.at[g], (left_mix if way == 0 else right_mix).at[g],
            mx_s.at[lax.rem(g, RING), way], mx_r.at[lax.rem(g, RING), way], device(0, 1 - 2 * way))

    def mf_copy(g, way):
        part = pl.ds(way * HALF, HALF)
        return remote(
            (left_mix if way == 0 else right_mix).at[g, part], far_mix.at[g, part],
            mf_s.at[lax.rem(g, RING), way], mf_r.at[lax.rem(g, RING), way], device(0, 1 - 2 * way))

    def mz_copy(g, way):
        return remote(
            (left_mix if way == 0 else right_mix).at[g], (below if way == 0 else above).at[g],
            mz_s.at[lax.rem(g, RING), way], mz_r.at[lax.rem(g, RING), way], device(1 - 2 * way, 0))

    def x_send(g):
        @pl.when(g >= RING)
        def _():
            for way in range(2):
                mx_copy(g - RING, way).wait_send()

        for way in range(2):
            mx_copy(g, way).start()

    def x_pass(g):
        for way in range(2):
            mx_copy(g, way).wait_recv()
            mf_copy(g, way).start()

    def z_send(g):
        for way in range(2):
            mf_copy(g, way).wait_recv()
            mf_copy(g, way).wait_send()
        slot = lax.rem(g, 4)

        @pl.loop(0, 4)
        def _(piece):
            rows = pl.ds(pl.multiple_of(piece * (COLS // 4), 16), COLS // 4)
            parts = [ref[g, rows, :].astype(f32) for ref in (own_mix, left_mix, right_mix, far_mix)]

            def weighted(shares):
                total = shares[0] * parts[0]
                for c, part in zip(shares[1:], parts[1:]):
                    total = total + c * part
                return total

            mine[slot, rows, :] = weighted(here_c)
            left_mix[g, rows, :] = weighted(up_c).astype(bf16)
            right_mix[g, rows, :] = weighted(down_c).astype(bf16)

        @pl.when(g >= RING)
        def _():
            for way in range(2):
                mz_copy(g - RING, way).wait_send()

        for way in range(2):
            mz_copy(g, way).start()

    def out_copy(out, i, slot):
        return pltpu.make_async_copy(
            staged.at[slot], out.at[:, pl.ds(pl.multiple_of(i * CH, CH), CH)], out_sem.at[slot])

    def finish(out, i, g):
        for way in range(2):
            mz_copy(g, way).wait_recv()
        total = mine[lax.rem(g, 4)] + below[g].astype(f32) + above[g].astype(f32)
        slot = lax.rem(g, 2)

        @pl.when(g >= 2)
        def _():
            out_copy(out, i, slot).wait()

        staged[slot] = total.astype(bf16)
        out_copy(out, i, slot).start()

    produce(0, 0)
    x_send(0)
    produce(0, 1)
    x_send(1)
    x_pass(0)

    @pl.loop(0, 2 * NC + 2)
    def _(g):
        ahead = (g + 4) // 2

        @pl.when((lax.rem(g, 2) == 0) & (ahead < NC // 2))
        def _():
            produce(0, ahead)

        @pl.when((lax.rem(g, 2) == 0) & (ahead >= NC // 2) & (ahead < NC))
        def _():
            produce(1, ahead - NC // 2)

        @pl.when(g + 2 < 2 * NC)
        def _():
            x_send(g + 2)

        @pl.when(g + 1 < 2 * NC)
        def _():
            x_pass(g + 1)

        @pl.when(g < 2 * NC)
        def _():
            z_send(g)

        for lag, tangent_step in enumerate(tangent_steps):
            @pl.when((g >= lag) & (g < lag + 4))
            def _(lag=lag, tangent_step=tangent_step):
                tangent_step(g - lag)

        @pl.when(g == len(tangent_steps) + 3)
        def _():
            tangent_gates()

        @pl.when((g >= 2) & (g < NC + 2))
        def _():
            finish(out_w, g - 2, g - 2)

        @pl.when(g >= NC + 2)
        def _():
            finish(out_t, g - 2 - NC, g - 2)

    for slot in range(2):
        out_copy(out_t, 0, slot).wait()
    up_gather.drain()
    down_gather.drain()
    target_copy.wait_send()

    tk_wait(7, 0, 0).wait_send()
    tk_wait(8, 1, 0).wait_send()

    blocks_wait(rs_recv.at[0, :, pl.ds(0, 7)], rs_s.at[0], rs_r.at[0, 0]).wait_send()
    blocks_wait(rs_recv.at[0, :, pl.ds(0, 7)], ag_s.at[0], ag_r.at[0, 0]).wait_send()
    blocks_wait(rs_recv.at[1, :, pl.ds(0, 6)], rs_s.at[1], rs_r.at[1, 0]).wait_send()
    blocks_wait(rs_recv.at[1, :, pl.ds(0, 7)], ag_s.at[1], ag_r.at[1, 0]).wait_send()
    blocks_wait(pair_send, pair_s, pair_r.at[0]).wait_send()
    blocks_wait(core_send, cs_s, cs_r.at[0, 0]).wait_send()
    blocks_wait(core_send, ac_s, ac_r.at[0, 0]).wait_send()
    for g in range(2 * NC - RING, 2 * NC):
        for way in range(2):
            mx_copy(g, way).wait_send()
            mz_copy(g, way).wait_send()


def local(
    tokens, targets, gate_weight, probes, tracker, up_weight, down_weight, neighbours, numerators
):
    vmem = pl.BlockSpec(memory_space=pltpu.VMEM)
    hbm = pl.BlockSpec(memory_space=pl.ANY)
    dma = pltpu.SemaphoreType.DMA
    weight = jax.ShapeDtypeStruct((COLS, D), bf16)
    wide = pltpu.VMEM((TOK, COLS), f32)
    turned = pltpu.VMEM((COLS, TOK), f32)
    mixed = pltpu.VMEM((2 * NC, COLS, CH), bf16)
    gather_sems = [dma((3,)), dma((2,)), dma, dma((4, 2)), dma((4,))]
    mixed_weights, mixed_tracker = pl.pallas_call(
        kernel,
        out_shape=(weight, weight),
        in_specs=[vmem, vmem, hbm, hbm, hbm, hbm, hbm, hbm, hbm],
        out_specs=(hbm, hbm),
        scratch_shapes=[
            pltpu.SMEM((6, 16), jnp.int32),
            pltpu.SMEM((6, 16), jnp.int32),
            pltpu.VMEM((COLS, D), bf16),
            pltpu.VMEM((COLS, D), bf16),
            pltpu.VMEM((COLS, D), bf16),
            pltpu.VMEM((16, 48, 1024), bf16),
            pltpu.VMEM((2, 48, 1024), bf16),
            pltpu.VMEM((TOK, D), bf16),
            pltpu.VMEM((4, 4, COLS, 128), bf16),
            pltpu.VMEM((4, 4, COLS, 128), bf16),
            wide, wide, wide, turned, turned, turned, turned,
            pltpu.VMEM((2, TOK, COLS), bf16),
            pltpu.VMEM((2, COLS, TOK), bf16),
            pltpu.VMEM((2, 4, TOK, 256), bf16),
            pltpu.VMEM((2, 4, TOK, 256), bf16),
            pltpu.VMEM((2, 4, TOK, 256), f32),
            pltpu.VMEM((2, 4, 2, TOK // 2, 256), bf16),
            pltpu.VMEM((2, 4, 8, 48, 256), bf16),
            pltpu.VMEM((4, 48, 256), bf16),
            pltpu.VMEM((4, 48, 256), bf16),
            pltpu.VMEM((2, 4, 2, TOK, 256), bf16),
            mixed, mixed, mixed, mixed, mixed, mixed,
            pltpu.VMEM((4, COLS, CH), f32),
            pltpu.VMEM((2, COLS, CH), bf16),
            dma((7,)), dma((2,)), dma((4,)), dma, dma,
            *gather_sems, *gather_sems,
            dma, dma((2, 4)), dma((2,)), dma((2, 4)), dma, dma((4,)),
            dma((2,)), dma((2, 4)), dma((4,)), dma, dma((2, 4)),
            dma((RING, 2)), dma((RING, 2)), dma((RING, 2)), dma((RING, 2)),
            dma((RING, 2)), dma((RING, 2)), dma((2,)),
        ],
        compiler_params=pltpu.CompilerParams(
            collective_id=0, has_side_effects=True, vmem_limit_bytes=63 << 20
        ),
        name="step_and_mix",
    )(
        tokens[0], targets[0], gate_weight[0].T, probes[0].T, tracker[0].T, up_weight.T, down_weight,
        neighbours.T, numerators.T,
    )
    return (mixed_weights.T[None], mixed_tracker.T[None])


def solution(mesh):
    return jax.shard_map(
        local,
        mesh=mesh,
        in_specs=(
            P("replica", "tensor", None),
            P("replica", "tensor", None),
            P("replica", None, "tensor"),
            P("replica", None, "tensor"),
            P("replica", None, "tensor"),
            P("replica", "tensor"),
            P("tensor", "replica"),
            P(),
            P(),
        ),
        out_specs=(P("replica", None, "tensor"), P("replica", None, "tensor")),
        check_vma=False,
    )
```

```python
import functools
import math

import jax
import jax.numpy as jnp
from jax import lax
from jax.experimental import pallas as pl
from jax.experimental.pallas import tpu as pltpu
from jax.sharding import PartitionSpec as P

MESH = pl.DeviceIdType.MESH
D = 2048
FF = 7168
DEN = 64
TOK = 384
COLS = 448
STEP_SIZE = 0.1
FLOOR = 0.1
DECAY = 0.75
INV_WIDTH = 1.0 / math.sqrt(D)
INV_HIDDEN = 1.0 / math.sqrt(FF)

CH = 128
NC = D // CH
HALF = COLS // 2
FIRST_Z = 352
RING = 8
f32 = jnp.float32
bf16 = jnp.bfloat16


def mod(value, count):
    return lax.rem(value + 4 * count, count)


class Gather:
    first, rows = 0, FIRST_Z

    def __init__(self, ref, own, sems, zh, x, device):
        self.ref, self.own, self.zh, self.x, self.device = ref, own.at[pl.ds(self.first, self.rows)], zh, x, device
        (self.sent, self.z_r, self.zf_r, self.x_r, self.xf_r) = sems

    def slot(self, column, row):
        return self.ref.at[row, column, pl.ds(self.first, self.rows)]

    def part(self, column, row, half):
        size = self.rows // 2
        return self.ref.at[row, column, pl.ds(self.first + half * size, size)]

    def copy(self, src, dst, send, recv, dz, dx):
        return pltpu.make_async_remote_copy(
            src, dst, self.sent.at[send], recv, device_id=self.device(dz, dx), device_id_type=MESH)

    def z_copy(self, way):
        return self.copy(self.own, self.slot(self.x, self.zh), 0, self.z_r.at[way], 1 - 2 * way, 0)

    def z_start(self):
        for way in range(2):
            self.z_copy(way).start()

    def z_forward(self):
        for way in range(2):
            self.z_copy(way).wait_recv()
            block = self.part(self.x, mod(self.zh - (1 - 2 * way), 4), way)
            self.copy(block, block, 0, self.zf_r, 1 - 2 * way, 0).start()

    def whole(self, block, send, recv):
        return self.copy(block, block, send, recv, 1, 0)

    def z_last(self):
        self.whole(self.slot(self.x, mod(self.zh + 2, 4)), 0, self.zf_r).wait_recv()

    def x_copy(self, q, way):
        block = self.slot(self.x, mod(self.zh + q, 4))
        return self.copy(self.own if q == 0 else block, block, 1, self.x_r.at[q, way], 0, 1 - 2 * way)

    def x_start(self, q):
        for way in range(2):
            self.x_copy(q, way).start()

    def x_forward(self, q):
        for way in range(2):
            self.x_copy(q, way).wait_recv()
            block = self.part(mod(self.x - (1 - 2 * way), 4), mod(self.zh + q, 4), way)
            self.copy(block, block, 2, self.xf_r.at[q], 0, 1 - 2 * way).start()

    def x_last(self, q):
        self.whole(self.slot(mod(self.x + 2, 4), mod(self.zh + q, 4)), 2, self.xf_r.at[q]).wait_recv()

    def drain(self):
        rows = pl.ds(self.first, self.rows)
        sent = (self.ref.at[0, pl.ds(0, 3), rows], self.ref.at[pl.ds(0, 2), :, rows], self.ref.at[0, :, rows])
        for i, blocks in enumerate(sent):
            self.whole(blocks, i, self.zf_r).wait_send()


class RowGather(Gather):
    first, rows = FIRST_Z, COLS - FIRST_Z

    def x_copy(self, way):
        return self.copy(self.own, self.slot(self.x, self.zh), 0, self.x_r.at[way], 0, 1 - 2 * way)

    def x_start(self):
        for way in range(2):
            self.x_copy(way).start()

    def x_forward(self):
        for way in range(2):
            self.x_copy(way).wait_recv()
            block = self.part(mod(self.x - (1 - 2 * way), 4), self.zh, way)
            self.copy(block, block, 0, self.xf_r, 0, 1 - 2 * way).start()

    def x_last(self):
        self.whole(self.slot(mod(self.x + 2, 4), self.zh), 0, self.xf_r).wait_recv()

    def z_copy(self, way):
        blocks = self.ref.at[self.zh, :, pl.ds(self.first, self.rows)]
        return self.copy(blocks, blocks, 1, self.z_r.at[way], 1 - 2 * way, 0)

    def z_forward(self):
        size = self.rows // 2
        for way in range(2):
            self.z_copy(way).wait_recv()
            blocks = self.ref.at[mod(self.zh - (1 - 2 * way), 4), :, pl.ds(self.first + way * size, size)]
            self.copy(blocks, blocks, 1, self.zf_r, 1 - 2 * way, 0).start()

    def z_last(self):
        blocks = self.ref.at[mod(self.zh + 2, 4), :, pl.ds(self.first, self.rows)]
        self.whole(blocks, 1, self.zf_r).wait_recv()

    def drain(self):
        rows = pl.ds(self.first, self.rows)
        for i, blocks in enumerate((self.ref.at[0, pl.ds(0, 3), rows], self.ref.at[pl.ds(0, 3), :, rows])):
            self.whole(blocks, i, self.zf_r).wait_send()


def kernel(
    tok_ref, tgt_ref, w_hbm, p_hbm, h_hbm, up_ref, down_ref, nb_hbm, num_hbm,
    out_w, out_t,
    nb_ref, num_ref,
    w_ref, p_ref, h_ref, tk, pair, x_all, upb, dnb,
    gate_acc, probe_acc, up_acc, first_turned, second_turned, grad_acc, tang_acc,
    hid, gates, core_send, core_recv, own_part, rs_send, rs_recv, pair_send, pair_recv, res,
    own_mix, left_mix, right_mix, far_mix, below, above, mine, staged,
    load_sem, tk_s, tk_r, tg_s, tg_r,
    u_s, uz_r, uzf_r, ux_r, uxf_r,
    d_s, dz_r, dzf_r, dx_r, dxf_r,
    ru_s, ruz_r, ruzf_r, rux_r, ruxf_r,
    rd_s, rdz_r, rdzf_r, rdx_r, rdxf_r,
    cs_s, cs_r, rs_s, rs_r, pair_s, pair_r, ag_s, ag_r, agp_r, ac_s, ac_r,
    mx_s, mx_r, mf_s, mf_r, mz_s, mz_r, out_sem,
):
    r = lax.axis_index("replica")
    t = lax.axis_index("tensor")
    zh, x = r // 4, lax.rem(r, 4)
    chip, core = t // 2, lax.rem(t, 2)
    half, y = chip // 4, lax.rem(chip, 4)
    sibling = (r, 2 * chip + 1 - core)

    def replica_at(dz, dx):
        return mod(zh + dz, 4) * 4 + mod(x + dx, 4)

    def device(dz, dx):
        return (replica_at(dz, dx), t)

    def peer(j):
        return (r, 2 * lax.rem(chip + j, 8) + core)

    def chip_at(a, b):
        return 4 * lax.rem(half + a, 2) + mod(y + b, 4)

    def same_core(a, b):
        return (r, 2 * chip_at(a, b) + core)

    def remote(src, dst, send, recv, where):
        return pltpu.make_async_remote_copy(
            src, dst, send, recv, device_id=where, device_id_type=MESH)

    barrier = pltpu.get_barrier_semaphore()
    partners = [device(1, 0), device(-1, 0), device(0, 1), device(0, -1), sibling]
    for where in partners:
        pl.semaphore_signal(barrier, inc=1, device_id=where, device_id_type=MESH)

    @pl.loop(1, 8)
    def _(j):
        pl.semaphore_signal(barrier, inc=1, device_id=peer(j), device_id_type=MESH)

    locals_in = (
        (up_ref, upb.at[zh, x]), (down_ref, dnb.at[zh, x]), (w_hbm, w_ref), (p_hbm, p_ref),
        (h_hbm, h_ref), (nb_hbm, nb_ref), (num_hbm, num_ref),
    )
    loads = [
        pltpu.make_async_copy(src, dst, load_sem.at[i]) for i, (src, dst) in enumerate(locals_in)
    ]
    for load in loads:
        load.start()

    def packed_rows(ref):
        block = ref[...].astype(f32)
        return jnp.concatenate([block[:, :1024], block[:, 1024:]], axis=0).astype(bf16)

    tk[t] = packed_rows(tok_ref)
    pair[core] = packed_rows(tgt_ref)
    pl.semaphore_wait(barrier, 12)

    def tk_slot(a, b):
        return tk.at[2 * chip_at(a, b) + core]

    def tk_copy(a, b):
        block = tk_slot(a, 0) if b else tk_slot(0, 0)
        where = same_core(0, b) if b else same_core(1, 0)
        return remote(block, block, tk_s.at[0], tk_r.at[2 * a + (b > 0)], where)

    def tk_pass(a, b):
        block = tk_slot(a, -b)
        return remote(block, block, tk_s.at[1], tk_r.at[0], sibling)

    def tk_wait(count, send, recv):
        return remote(tk.at[pl.ds(0, count)], tk.at[pl.ds(0, count)], tk_s.at[send], tk_r.at[recv], sibling)

    target_copy = remote(pair.at[core], pair.at[core], tg_s, tg_r, sibling)

    up_gather = Gather(upb, up_ref, (u_s, uz_r, uzf_r, ux_r, uxf_r), zh, x, device)
    down_gather = Gather(dnb, down_ref, (d_s, dz_r, dzf_r, dx_r, dxf_r), zh, x, device)
    up_other = RowGather(upb, up_ref, (ru_s, ruz_r, ruzf_r, rux_r, ruxf_r), zh, x, device)
    down_other = RowGather(dnb, down_ref, (rd_s, rdz_r, rdzf_r, rdx_r, rdxf_r), zh, x, device)

    tk_copy(1, 0).start()
    for b in range(1, 4):
        tk_copy(0, b).start()
    up_gather.z_start()
    up_other.x_start()
    up_gather.x_start(0)
    tk_pass(0, 0).start()
    target_copy.start()

    tk_copy(1, 0).wait_recv()
    for b in range(1, 4):
        tk_copy(1, b).start()
    tk_pass(1, 0).start()
    up_other.x_forward()
    down_other.x_start()
    down_gather.x_start(0)
    up_gather.x_forward(0)
    up_gather.z_forward()
    up_gather.x_start(1)
    up_gather.x_start(3)
    loads[0].wait()
    up_other.x_last()
    up_other.z_start()
    down_other.x_forward()
    tk_wait(3, 0, 1).wait_recv()
    for b in range(1, 4):
        tk_pass(0, b).start()
    up_gather.z_last()
    up_gather.x_start(2)
    down_gather.z_start()
    down_gather.x_forward(0)
    tk_wait(3, 0, 3).wait_recv()
    for b in range(1, 4):
        tk_pass(1, b).start()
    up_gather.x_forward(1)
    tk_wait(8, 1, 0).wait_recv()

    @pl.loop(0, 8)
    def _(c):
        blocks = [tk[2 * c + k].astype(f32) for k in range(2)]
        rows = [jnp.concatenate([b[:24], b[24:]], axis=1) for b in blocks]
        x_all[pl.ds(pl.multiple_of(c * 48, 48), 48), :] = jnp.concatenate(rows, axis=0).astype(bf16)

    up_gather.x_forward(3)
    up_other.z_forward()

    def joined(ref, row, first, count):
        return jnp.concatenate([ref[row, first + i] for i in range(count)], axis=1)

    def rows_dot(left, right):
        return lax.dot_general(left, right, (((1,), (1,)), ((), ())), preferred_element_type=f32)

    def wide_dot(acc, weight):
        acc[...] = rows_dot(x_all[...], weight[...])

    loads[2].wait()
    wide_dot(gate_acc, w_ref)
    up_gather.x_forward(2)
    down_gather.z_forward()
    down_gather.x_start(1)
    down_gather.x_start(3)
    loads[1].wait()
    down_other.x_last()
    down_other.z_start()
    loads[3].wait()
    wide_dot(probe_acc, p_ref)

    def up_rows(q):
        row = mod(zh + q, 4)
        return rows_dot(x_all[:, pl.ds(pl.multiple_of(512 * row, 512), 512)], joined(upb, row, 0, 4))

    for q in (0, 1, 3):
        up_gather.x_last(q)
    up_other.z_last()
    up_acc[...] = up_rows(0) + up_rows(1) + up_rows(3)
    up_gather.x_last(2)
    up_acc[...] += up_rows(2)
    down_gather.z_last()
    down_gather.x_start(2)

    @pl.loop(0, 8)
    def _(c):
        rows = pl.ds(pl.multiple_of(c * 48, 48), 48)
        gate_pre = gate_acc[rows, :] * INV_WIDTH
        probe_pre = probe_acc[rows, :] * INV_WIDTH
        up_pre = up_acc[rows, :] * INV_WIDTH
        logistic = jax.nn.sigmoid(gate_pre)
        slope_one = logistic * (1.0 + gate_pre * (1.0 - logistic))
        slope_two = logistic * (1.0 - logistic) * (2.0 + gate_pre * (1.0 - 2.0 * logistic))
        hid[0, rows, :] = (gate_pre * logistic * up_pre).astype(bf16)
        first = up_pre * slope_one
        hid[1, rows, :] = (first * probe_pre).astype(bf16)
        gate_acc[rows, :] = first
        probe_acc[rows, :] = up_pre * slope_two * probe_pre

    target_copy.wait_recv()
    down_gather.x_forward(1)
    down_other.z_forward()

    order = (0, 1, 3, 2)

    def column(s, p):
        return mod(zh + order[s], 4) if p == 0 else lax.rem(zh + s, 4)

    def core_copy(s, p):
        return remote(core_send.at[p, s], core_recv.at[p, s], cs_s, cs_r.at[p, s], sibling)

    def forward(s, p):
        away = jnp.dot(hid[p], joined(dnb, column(s, p), 2 * (1 - core), 2), preferred_element_type=f32)
        core_send[p, s] = (away * INV_HIDDEN).astype(bf16)
        core_copy(s, p).start()
        here = jnp.dot(hid[p], joined(dnb, column(s, p), 2 * core, 2), preferred_element_type=f32)
        own_part[p, s] = here * INV_HIDDEN

    def blocks_wait(blocks, send, recv):
        return remote(blocks, blocks, send, recv, sibling)

    def rs_copy(s, p, j):
        to = lax.rem(chip + j, 8)
        return remote(
            rs_send.at[p, s, to // 4, pl.ds(pl.multiple_of(48 * lax.rem(to, 4), 48), 48)], rs_recv.at[p, s, j],
            rs_s.at[p], rs_r.at[p, s], peer(j))

    def core_sum(s, p):
        core_copy(s, p).wait_recv()
        total = own_part[p, s] + core_recv[p, s].astype(f32)
        own_part[p, s] = total
        rs_send[p, s] = total.astype(bf16).reshape(2, TOK // 2, 256)

    def scatter(s, p):
        core_sum(s, p)

        @pl.loop(1, 8)
        def _(j):
            rs_copy(s, p, j).start()

    own_rows = pl.ds(pl.multiple_of(48 * chip, 48), 48)

    def ag_copy(s, p, j):
        block = res.at[p, s, core, own_rows]
        return remote(block, block, ag_s.at[p], ag_r.at[p, s], peer(j))

    def reduce(s, p):
        blocks_wait(rs_recv.at[p, s, pl.ds(1, 7)], rs_s.at[p], rs_r.at[p, s]).wait_recv()
        total = own_part[p, s, own_rows, :]
        for j in range(1, 8):
            total = total + rs_recv[p, s, j].astype(f32)
        row = column(s, p)
        at = pl.ds(pl.multiple_of(512 * lax.rem(row, 2) + 256 * core, 256), 256)
        target = []
        for k in range(2):
            both = pair[k, :, at].astype(f32)
            target.append(jnp.where(row < 2, both[:24], both[24:]))
        total = total - jnp.concatenate(target, axis=0)
        res[p, s, core, own_rows, :] = total.astype(bf16)

        @pl.loop(1, 8)
        def _(j):
            ag_copy(s, p, j).start()

    def across_copy(s, p, k):
        return remote(res.at[p, s, k], res.at[p, s, k], ac_s, ac_r.at[p, s], sibling)

    def across(s, p):
        blocks_wait(rs_recv.at[p, s, pl.ds(1, 7)], ag_s.at[p], ag_r.at[p, s]).wait_recv()
        across_copy(s, p, core).start()

    def backward(s, p, acc):
        across_copy(s, p, 1 - core).wait_recv()
        rows = jnp.concatenate([res[p, s, 0], res[p, s, 1]], axis=1)
        part = rows_dot(joined(dnb, column(s, p), 0, 4), rows) * INV_HIDDEN
        if p == 0 and s == 0:
            acc[...] = part
        else:
            acc[...] += part

    def y_copy(s, b):
        rows = pl.ds(pl.multiple_of(48 * mod(y + b, 4), 48), 48)
        return remote(
            rs_send.at[1, s, :, rows], rs_recv.at[1, s, pl.ds(2 * b, 2)],
            rs_s.at[1], rs_r.at[1, s], same_core(0, b))

    def pair_copy(s):
        return remote(pair_send.at[s], pair_recv.at[s], pair_s, pair_r.at[s], same_core(1, 0))

    def y_scatter(s):
        core_sum(s, 1)
        for b in range(1, 4):
            y_copy(s, b).start()

    def y_reduce(s):
        blocks_wait(rs_recv.at[1, s, pl.ds(2, 6)], rs_s.at[1], rs_r.at[1, s]).wait_recv()

        def total(at):
            value = own_part[1, s, pl.ds(pl.multiple_of(48 * (4 * at + y), 48), 48), :]
            for b in range(1, 4):
                value = value + rs_recv[1, s, 2 * b + at].astype(f32)
            return value

        pair_send[s] = total(1 - half).astype(bf16)
        pair_copy(s).start()
        own_part[1, s, own_rows, :] = total(half)

    def t_copy(s, a, b):
        at = chip_at(a, 0) if b else chip
        block = res.at[1, s, core, pl.ds(pl.multiple_of(48 * at, 48), 48)]
        where = same_core(0, b) if b else same_core(1, 0)
        return remote(block, block, ag_s.at[1], ag_r.at[1, s] if b else agp_r.at[s], where)

    def pair_reduce(s):
        pair_copy(s).wait_recv()
        total = own_part[1, s, own_rows, :] + pair_recv[s].astype(f32)
        res[1, s, core, own_rows, :] = total.astype(bf16)
        t_copy(s, 1, 0).start()
        for b in range(1, 4):
            t_copy(s, 0, b).start()

    def pair_pass(s):
        t_copy(s, 1, 0).wait_recv()
        for b in range(1, 4):
            t_copy(s, 1, b).start()

    def t_across(s):
        blocks_wait(rs_recv.at[1, s, pl.ds(2, 6)], ag_s.at[1], ag_r.at[1, s]).wait_recv()
        across_copy(s, 1, core).start()

    def turn(p):
        source, turned = ((gate_acc, first_turned), (probe_acc, second_turned))[p]

        @pl.loop(0, 3)
        def _(c):
            tokens_at = pl.ds(pl.multiple_of(c * 128, 128), 128)
            turned[:, tokens_at] = source[tokens_at, :].T

    def ready(s):
        down_gather.x_last(order[s])
        if s == 3:
            down_other.z_last()

    def sums(s):
        ready(s)
        forward(s, 0)

    sums(0)
    down_gather.x_forward(3)
    sums(1)
    scatter(0, 0)
    scatter(1, 0)
    down_gather.x_forward(2)
    sums(2)
    reduce(0, 0)
    scatter(2, 0)
    sums(3)
    reduce(1, 0)
    scatter(3, 0)
    across(0, 0)
    turn(0)
    reduce(2, 0)
    backward(0, 0, grad_acc)
    across(1, 0)
    turn(1)
    reduce(3, 0)
    backward(1, 0, grad_acc)
    across(2, 0)
    backward(2, 0, grad_acc)
    across(3, 0)
    backward(3, 0, grad_acc)

    loads[4].wait()
    tang_acc[...] = jnp.zeros_like(tang_acc)

    @pl.loop(0, 7)
    def _(c):
        rows = pl.ds(pl.multiple_of(c * 64, 64), 64)
        gates[0, rows, :] = (grad_acc[rows, :] * first_turned[rows, :]).astype(bf16)

    def tangent_gates():
        @pl.loop(0, 7)
        def _(c):
            rows = pl.ds(pl.multiple_of(c * 64, 64), 64)
            gates[1, rows, :] = (
                tang_acc[rows, :] * first_turned[rows, :] + grad_acc[rows, :] * second_turned[rows, :]
            ).astype(bf16)

    tangent_steps = (
        lambda s: forward(s, 1),
        y_scatter,
        y_reduce,
        pair_reduce,
        pair_pass,
        t_across,
        lambda s: backward(s, 1, tang_acc),
    )

    def share(dest, source):
        total = jnp.int32(0)
        for k in range(6):
            total = total + jnp.where(nb_ref[k, dest] == source, num_ref[k, dest], 0)
        return total.astype(f32) * (1.0 / DEN)

    def self_share():
        total = jnp.int32(0)
        for k in range(6):
            total = total + num_ref[k, r]
        return (DEN - total).astype(f32) * (1.0 / DEN)

    loads[5].wait()
    loads[6].wait()
    sources = [replica_at(0, dx) for dx in (0, -1, 1, 2)]
    here_c = [self_share()] + [share(r, source) for source in sources[1:]]
    up_c = [share(replica_at(1, 0), source) for source in sources]
    down_c = [share(replica_at(-1, 0), source) for source in sources]

    def produce(path, pair_at):
        lanes = pl.ds(pl.multiple_of(pair_at * 256, 256), 256)
        change = jnp.dot(gates[path], x_all[:, lanes], preferred_element_type=f32) * INV_WIDTH
        old = h_ref[:, lanes].astype(f32)
        if path == 0:
            ratio = change / jnp.maximum(old, FLOOR)
            new = w_ref[:, lanes].astype(f32) - STEP_SIZE * jnp.clip(ratio, -1.0, 1.0)
        else:
            new = DECAY * old + (1.0 - DECAY) * p_ref[:, lanes].astype(f32) * change
        for m in range(2):
            own_mix[path * NC + 2 * pair_at + m] = new[:, 128 * m : 128 * (m + 1)].astype(bf16)

    def mx_copy(g, way):
        return remote(
            own_mix.at[g], (left_mix if way == 0 else right_mix).at[g],
            mx_s.at[lax.rem(g, RING), way], mx_r.at[lax.rem(g, RING), way], device(0, 1 - 2 * way))

    def mf_copy(g, way):
        part = pl.ds(way * HALF, HALF)
        return remote(
            (left_mix if way == 0 else right_mix).at[g, part], far_mix.at[g, part],
            mf_s.at[lax.rem(g, RING), way], mf_r.at[lax.rem(g, RING), way], device(0, 1 - 2 * way))

    def mz_copy(g, way):
        return remote(
            (left_mix if way == 0 else right_mix).at[g], (below if way == 0 else above).at[g],
            mz_s.at[lax.rem(g, RING), way], mz_r.at[lax.rem(g, RING), way], device(1 - 2 * way, 0))

    def x_send(g):
        @pl.when(g >= RING)
        def _():
            for way in range(2):
                mx_copy(g - RING, way).wait_send()

        for way in range(2):
            mx_copy(g, way).start()

    def x_pass(g):
        for way in range(2):
            mx_copy(g, way).wait_recv()
            mf_copy(g, way).start()

    def z_send(g):
        for way in range(2):
            mf_copy(g, way).wait_recv()
            mf_copy(g, way).wait_send()
        slot = lax.rem(g, 4)

        @pl.loop(0, 4)
        def _(piece):
            rows = pl.ds(pl.multiple_of(piece * (COLS // 4), 16), COLS // 4)
            parts = [ref[g, rows, :].astype(f32) for ref in (own_mix, left_mix, right_mix, far_mix)]

            def weighted(shares):
                total = shares[0] * parts[0]
                for c, part in zip(shares[1:], parts[1:]):
                    total = total + c * part
                return total

            mine[slot, rows, :] = weighted(here_c)
            left_mix[g, rows, :] = weighted(up_c).astype(bf16)
            right_mix[g, rows, :] = weighted(down_c).astype(bf16)

        @pl.when(g >= RING)
        def _():
            for way in range(2):
                mz_copy(g - RING, way).wait_send()

        for way in range(2):
            mz_copy(g, way).start()

    def out_copy(out, i, slot):
        return pltpu.make_async_copy(
            staged.at[slot], out.at[:, pl.ds(pl.multiple_of(i * CH, CH), CH)], out_sem.at[slot])

    def finish(out, i, g):
        for way in range(2):
            mz_copy(g, way).wait_recv()
        total = mine[lax.rem(g, 4)] + below[g].astype(f32) + above[g].astype(f32)
        slot = lax.rem(g, 2)

        @pl.when(g >= 2)
        def _():
            out_copy(out, i, slot).wait()

        staged[slot] = total.astype(bf16)
        out_copy(out, i, slot).start()

    produce(0, 0)
    x_send(0)
    produce(0, 1)
    x_send(1)
    x_pass(0)

    @pl.loop(0, 2 * NC + 2)
    def _(g):
        ahead = (g + 4) // 2

        @pl.when((lax.rem(g, 2) == 0) & (ahead < NC // 2))
        def _():
            produce(0, ahead)

        @pl.when((lax.rem(g, 2) == 0) & (ahead >= NC // 2) & (ahead < NC))
        def _():
            produce(1, ahead - NC // 2)

        @pl.when(g + 2 < 2 * NC)
        def _():
            x_send(g + 2)

        @pl.when(g + 1 < 2 * NC)
        def _():
            x_pass(g + 1)

        @pl.when(g < 2 * NC)
        def _():
            z_send(g)

        for lag, tangent_step in enumerate(tangent_steps):
            @pl.when((g >= lag) & (g < lag + 4))
            def _(lag=lag, tangent_step=tangent_step):
                tangent_step(g - lag)

        @pl.when(g == len(tangent_steps) + 3)
        def _():
            tangent_gates()

        @pl.when((g >= 2) & (g < NC + 2))
        def _():
            finish(out_w, g - 2, g - 2)

        @pl.when(g >= NC + 2)
        def _():
            finish(out_t, g - 2 - NC, g - 2)

    for slot in range(2):
        out_copy(out_t, 0, slot).wait()
    up_gather.drain()
    down_gather.drain()
    up_other.drain()
    down_other.drain()
    target_copy.wait_send()

    tk_wait(7, 0, 0).wait_send()
    tk_wait(8, 1, 0).wait_send()

    blocks_wait(rs_recv.at[0, :, pl.ds(0, 7)], rs_s.at[0], rs_r.at[0, 0]).wait_send()
    blocks_wait(rs_recv.at[0, :, pl.ds(0, 7)], ag_s.at[0], ag_r.at[0, 0]).wait_send()
    blocks_wait(rs_recv.at[1, :, pl.ds(0, 6)], rs_s.at[1], rs_r.at[1, 0]).wait_send()
    blocks_wait(rs_recv.at[1, :, pl.ds(0, 7)], ag_s.at[1], ag_r.at[1, 0]).wait_send()
    blocks_wait(pair_send, pair_s, pair_r.at[0]).wait_send()
    blocks_wait(core_send, cs_s, cs_r.at[0, 0]).wait_send()
    blocks_wait(core_send, ac_s, ac_r.at[0, 0]).wait_send()
    for g in range(2 * NC - RING, 2 * NC):
        for way in range(2):
            mx_copy(g, way).wait_send()
            mz_copy(g, way).wait_send()


def local(
    tokens, targets, gate_weight, probes, tracker, up_weight, down_weight, neighbours, numerators
):
    vmem = pl.BlockSpec(memory_space=pltpu.VMEM)
    hbm = pl.BlockSpec(memory_space=pl.ANY)
    dma = pltpu.SemaphoreType.DMA
    weight = jax.ShapeDtypeStruct((COLS, D), bf16)
    wide = pltpu.VMEM((TOK, COLS), f32)
    turned = pltpu.VMEM((COLS, TOK), f32)
    mixed = pltpu.VMEM((2 * NC, COLS, CH), bf16)
    other_sems = [dma((2,)), dma((2,)), dma, dma((2,)), dma]
    gather_sems = [dma((3,)), dma((2,)), dma, dma((4, 2)), dma((4,))]
    mixed_weights, mixed_tracker = pl.pallas_call(
        kernel,
        out_shape=(weight, weight),
        in_specs=[vmem, vmem, hbm, hbm, hbm, hbm, hbm, hbm, hbm],
        out_specs=(hbm, hbm),
        scratch_shapes=[
            pltpu.SMEM((6, 16), jnp.int32),
            pltpu.SMEM((6, 16), jnp.int32),
            pltpu.VMEM((COLS, D), bf16),
            pltpu.VMEM((COLS, D), bf16),
            pltpu.VMEM((COLS, D), bf16),
            pltpu.VMEM((16, 48, 1024), bf16),
            pltpu.VMEM((2, 48, 1024), bf16),
            pltpu.VMEM((TOK, D), bf16),
            pltpu.VMEM((4, 4, COLS, 128), bf16),
            pltpu.VMEM((4, 4, COLS, 128), bf16),
            wide, wide, wide, turned, turned, turned, turned,
            pltpu.VMEM((2, TOK, COLS), bf16),
            pltpu.VMEM((2, COLS, TOK), bf16),
            pltpu.VMEM((2, 4, TOK, 256), bf16),
            pltpu.VMEM((2, 4, TOK, 256), bf16),
            pltpu.VMEM((2, 4, TOK, 256), f32),
            pltpu.VMEM((2, 4, 2, TOK // 2, 256), bf16),
            pltpu.VMEM((2, 4, 8, 48, 256), bf16),
            pltpu.VMEM((4, 48, 256), bf16),
            pltpu.VMEM((4, 48, 256), bf16),
            pltpu.VMEM((2, 4, 2, TOK, 256), bf16),
            mixed, mixed, mixed, mixed, mixed, mixed,
            pltpu.VMEM((4, COLS, CH), f32),
            pltpu.VMEM((2, COLS, CH), bf16),
            dma((7,)), dma((2,)), dma((4,)), dma, dma,
            *gather_sems, *gather_sems, *other_sems, *other_sems,
            dma, dma((2, 4)), dma((2,)), dma((2, 4)), dma, dma((4,)),
            dma((2,)), dma((2, 4)), dma((4,)), dma, dma((2, 4)),
            dma((RING, 2)), dma((RING, 2)), dma((RING, 2)), dma((RING, 2)),
            dma((RING, 2)), dma((RING, 2)), dma((2,)),
        ],
        compiler_params=pltpu.CompilerParams(
            collective_id=0, has_side_effects=True, vmem_limit_bytes=63 << 20
        ),
        name="step_and_mix",
    )(
        tokens[0], targets[0], gate_weight[0].T, probes[0].T, tracker[0].T, up_weight.T, down_weight,
        neighbours.T, numerators.T,
    )
    return (mixed_weights.T[None], mixed_tracker.T[None])


def solution(mesh):
    return jax.shard_map(
        local,
        mesh=mesh,
        in_specs=(
            P("replica", "tensor", None),
            P("replica", "tensor", None),
            P("replica", None, "tensor"),
            P("replica", None, "tensor"),
            P("replica", None, "tensor"),
            P("replica", "tensor"),
            P("tensor", "replica"),
            P(),
            P(),
        ),
        out_specs=(P("replica", None, "tensor"), P("replica", None, "tensor")),
        check_vma=False,
    )
```

```python
import functools
import math

import jax
import jax.numpy as jnp
from jax import lax
from jax.experimental import pallas as pl
from jax.experimental.pallas import tpu as pltpu
from jax.sharding import PartitionSpec as P

MESH = pl.DeviceIdType.MESH
D = 2048
FF = 7168
DEN = 64
TOK = 384
COLS = 448
STEP_SIZE = 0.1
FLOOR = 0.1
DECAY = 0.75
INV_WIDTH = 1.0 / math.sqrt(D)
INV_HIDDEN = 1.0 / math.sqrt(FF)

CH = 128
NC = D // CH
HALF = COLS // 2
FIRST_Z = 352
RING = 8
f32 = jnp.float32
bf16 = jnp.bfloat16


def mod(value, count):
    return lax.rem(value + 4 * count, count)


class Gather:
    first, rows = 0, FIRST_Z

    def __init__(self, ref, own, sems, zh, x, device):
        self.ref, self.own, self.zh, self.x, self.device = ref, own.at[pl.ds(self.first, self.rows)], zh, x, device
        (self.sent, self.z_r, self.zf_r, self.x_r, self.xf_r) = sems

    def slot(self, column, row):
        return self.ref.at[row, column, pl.ds(self.first, self.rows)]

    def part(self, column, row, half):
        size = self.rows // 2
        return self.ref.at[row, column, pl.ds(self.first + half * size, size)]

    def copy(self, src, dst, send, recv, dz, dx):
        return pltpu.make_async_remote_copy(
            src, dst, self.sent.at[send], recv, device_id=self.device(dz, dx), device_id_type=MESH)

    def z_copy(self, way):
        return self.copy(self.own, self.slot(self.x, self.zh), 0, self.z_r.at[way], 1 - 2 * way, 0)

    def z_start(self):
        for way in range(2):
            self.z_copy(way).start()

    def z_forward(self):
        for way in range(2):
            self.z_copy(way).wait_recv()
            block = self.part(self.x, mod(self.zh - (1 - 2 * way), 4), way)
            self.copy(block, block, 0, self.zf_r, 1 - 2 * way, 0).start()

    def whole(self, block, send, recv):
        return self.copy(block, block, send, recv, 1, 0)

    def z_last(self):
        self.whole(self.slot(self.x, mod(self.zh + 2, 4)), 0, self.zf_r).wait_recv()

    def x_copy(self, q, way):
        block = self.slot(self.x, mod(self.zh + q, 4))
        return self.copy(self.own if q == 0 else block, block, 1, self.x_r.at[q, way], 0, 1 - 2 * way)

    def x_start(self, q):
        for way in range(2):
            self.x_copy(q, way).start()

    def x_forward(self, q):
        for way in range(2):
            self.x_copy(q, way).wait_recv()
            block = self.part(mod(self.x - (1 - 2 * way), 4), mod(self.zh + q, 4), way)
            self.copy(block, block, 2, self.xf_r.at[q], 0, 1 - 2 * way).start()

    def x_last(self, q):
        self.whole(self.slot(mod(self.x + 2, 4), mod(self.zh + q, 4)), 2, self.xf_r.at[q]).wait_recv()

    def drain(self):
        rows = pl.ds(self.first, self.rows)
        sent = (self.ref.at[0, pl.ds(0, 3), rows], self.ref.at[pl.ds(0, 2), :, rows], self.ref.at[0, :, rows])
        for i, blocks in enumerate(sent):
            self.whole(blocks, i, self.zf_r).wait_send()


class RowGather(Gather):
    first, rows = FIRST_Z, COLS - FIRST_Z

    def x_copy(self, way):
        return self.copy(self.own, self.slot(self.x, self.zh), 0, self.x_r.at[way], 0, 1 - 2 * way)

    def x_start(self):
        for way in range(2):
            self.x_copy(way).start()

    def x_forward(self):
        for way in range(2):
            self.x_copy(way).wait_recv()
            block = self.part(mod(self.x - (1 - 2 * way), 4), self.zh, way)
            self.copy(block, block, 0, self.xf_r, 0, 1 - 2 * way).start()

    def x_last(self):
        self.whole(self.slot(mod(self.x + 2, 4), self.zh), 0, self.xf_r).wait_recv()

    def z_copy(self, way):
        blocks = self.ref.at[self.zh, :, pl.ds(self.first, self.rows)]
        return self.copy(blocks, blocks, 1, self.z_r.at[way], 1 - 2 * way, 0)

    def z_forward(self):
        size = self.rows // 2
        for way in range(2):
            self.z_copy(way).wait_recv()
            blocks = self.ref.at[mod(self.zh - (1 - 2 * way), 4), :, pl.ds(self.first + way * size, size)]
            self.copy(blocks, blocks, 1, self.zf_r, 1 - 2 * way, 0).start()

    def z_last(self):
        blocks = self.ref.at[mod(self.zh + 2, 4), :, pl.ds(self.first, self.rows)]
        self.whole(blocks, 1, self.zf_r).wait_recv()

    def drain(self):
        rows = pl.ds(self.first, self.rows)
        for i, blocks in enumerate((self.ref.at[0, pl.ds(0, 3), rows], self.ref.at[pl.ds(0, 3), :, rows])):
            self.whole(blocks, i, self.zf_r).wait_send()


def kernel(
    tok_ref, tgt_ref, w_hbm, p_hbm, h_hbm, up_ref, down_ref, nb_hbm, num_hbm,
    out_w, out_t,
    nb_ref, num_ref,
    w_ref, p_ref, h_ref, tk, pair, x_all, upb, dnb,
    gate_acc, probe_acc, up_acc, first_turned, second_turned, grad_acc, tang_acc,
    hid, gates, core_send, core_recv, own_part, rs_send, rs_recv, pair_send, pair_recv, res,
    own_mix, left_mix, right_mix, far_mix, below, above, mine, staged,
    load_sem, tk_s, tk_r, tg_s, tg_r,
    u_s, uz_r, uzf_r, ux_r, uxf_r,
    d_s, dz_r, dzf_r, dx_r, dxf_r,
    ru_s, ruz_r, ruzf_r, rux_r, ruxf_r,
    rd_s, rdz_r, rdzf_r, rdx_r, rdxf_r,
    cs_s, cs_r, rs_s, rs_r, pair_s, pair_r, ag_s, ag_r, agp_r, ac_s, ac_r,
    mx_s, mx_r, mf_s, mf_r, mz_s, mz_r, out_sem,
):
    r = lax.axis_index("replica")
    t = lax.axis_index("tensor")
    zh, x = r // 4, lax.rem(r, 4)
    chip, core = t // 2, lax.rem(t, 2)
    half, y = chip // 4, lax.rem(chip, 4)
    sibling = (r, 2 * chip + 1 - core)

    def replica_at(dz, dx):
        return mod(zh + dz, 4) * 4 + mod(x + dx, 4)

    def device(dz, dx):
        return (replica_at(dz, dx), t)

    def peer(j):
        return (r, 2 * lax.rem(chip + j, 8) + core)

    def chip_at(a, b):
        return 4 * lax.rem(half + a, 2) + mod(y + b, 4)

    def same_core(a, b):
        return (r, 2 * chip_at(a, b) + core)

    def remote(src, dst, send, recv, where):
        return pltpu.make_async_remote_copy(
            src, dst, send, recv, device_id=where, device_id_type=MESH)

    barrier = pltpu.get_barrier_semaphore()
    partners = [device(1, 0), device(-1, 0), device(0, 1), device(0, -1), sibling]
    for where in partners:
        pl.semaphore_signal(barrier, inc=1, device_id=where, device_id_type=MESH)

    @pl.loop(1, 8)
    def _(j):
        pl.semaphore_signal(barrier, inc=1, device_id=peer(j), device_id_type=MESH)

    locals_in = (
        (up_ref, upb.at[zh, x]), (down_ref, dnb.at[zh, x]), (w_hbm, w_ref), (p_hbm, p_ref),
        (h_hbm, h_ref), (nb_hbm, nb_ref), (num_hbm, num_ref),
    )
    loads = [
        pltpu.make_async_copy(src, dst, load_sem.at[i]) for i, (src, dst) in enumerate(locals_in)
    ]
    for load in loads:
        load.start()

    def packed_rows(ref):
        block = ref[...].astype(f32)
        return jnp.concatenate([block[:, :1024], block[:, 1024:]], axis=0).astype(bf16)

    tk[t] = packed_rows(tok_ref)
    pair[core] = packed_rows(tgt_ref)
    pl.semaphore_wait(barrier, 12)

    def tk_slot(a, b):
        return tk.at[2 * chip_at(a, b) + core]

    def tk_copy(a, b):
        block = tk_slot(a, 0) if b else tk_slot(0, 0)
        where = same_core(0, b) if b else same_core(1, 0)
        return remote(block, block, tk_s.at[0], tk_r.at[2 * a + (b > 0)], where)

    def tk_pass(a, b):
        block = tk_slot(a, -b)
        return remote(block, block, tk_s.at[1], tk_r.at[0], sibling)

    def tk_wait(count, send, recv):
        return remote(tk.at[pl.ds(0, count)], tk.at[pl.ds(0, count)], tk_s.at[send], tk_r.at[recv], sibling)

    target_copy = remote(pair.at[core], pair.at[core], tg_s, tg_r, sibling)

    up_gather = Gather(upb, up_ref, (u_s, uz_r, uzf_r, ux_r, uxf_r), zh, x, device)
    down_gather = Gather(dnb, down_ref, (d_s, dz_r, dzf_r, dx_r, dxf_r), zh, x, device)
    up_other = RowGather(upb, up_ref, (ru_s, ruz_r, ruzf_r, rux_r, ruxf_r), zh, x, device)
    down_other = RowGather(dnb, down_ref, (rd_s, rdz_r, rdzf_r, rdx_r, rdxf_r), zh, x, device)

    tk_copy(1, 0).start()
    for b in range(1, 4):
        tk_copy(0, b).start()
    up_gather.z_start()
    up_other.x_start()
    up_gather.x_start(0)
    tk_pass(0, 0).start()
    target_copy.start()

    tk_copy(1, 0).wait_recv()
    for b in range(1, 4):
        tk_copy(1, b).start()
    tk_pass(1, 0).start()
    up_other.x_forward()
    down_other.x_start()
    down_gather.x_start(0)
    up_gather.x_forward(0)
    up_gather.z_forward()
    up_gather.x_start(1)
    up_gather.x_start(3)
    loads[0].wait()
    up_other.x_last()
    up_other.z_start()
    down_other.x_forward()
    tk_wait(3, 0, 1).wait_recv()
    for b in range(1, 4):
        tk_pass(0, b).start()
    up_gather.z_last()
    up_gather.x_start(2)
    down_gather.z_start()
    down_gather.x_forward(0)
    tk_wait(3, 0, 3).wait_recv()
    for b in range(1, 4):
        tk_pass(1, b).start()
    up_gather.x_forward(1)
    tk_wait(8, 1, 0).wait_recv()

    @pl.loop(0, 8)
    def _(c):
        blocks = [tk[2 * c + k].astype(f32) for k in range(2)]
        rows = [jnp.concatenate([b[:24], b[24:]], axis=1) for b in blocks]
        x_all[pl.ds(pl.multiple_of(c * 48, 48), 48), :] = jnp.concatenate(rows, axis=0).astype(bf16)

    up_gather.x_forward(3)
    up_other.z_forward()

    def joined(ref, row, first, count):
        return jnp.concatenate([ref[row, first + i] for i in range(count)], axis=1)

    def rows_dot(left, right):
        return lax.dot_general(left, right, (((1,), (1,)), ((), ())), preferred_element_type=f32)

    def wide_dot(acc, weight):
        acc[...] = rows_dot(x_all[...], weight[...])

    loads[2].wait()
    wide_dot(gate_acc, w_ref)
    up_gather.x_forward(2)
    down_gather.z_forward()
    down_gather.x_start(1)
    down_gather.x_start(3)
    loads[1].wait()
    down_other.x_last()
    down_other.z_start()
    loads[3].wait()
    wide_dot(probe_acc, p_ref)

    def up_rows(q):
        row = mod(zh + q, 4)
        return rows_dot(x_all[:, pl.ds(pl.multiple_of(512 * row, 512), 512)], joined(upb, row, 0, 4))

    for q in (0, 1, 3):
        up_gather.x_last(q)
    up_other.z_last()
    up_acc[...] = up_rows(0) + up_rows(1) + up_rows(3)
    up_gather.x_last(2)
    up_acc[...] += up_rows(2)
    down_gather.z_last()
    down_gather.x_start(2)

    @pl.loop(0, 8)
    def _(c):
        rows = pl.ds(pl.multiple_of(c * 48, 48), 48)
        gate_pre = gate_acc[rows, :] * INV_WIDTH
        probe_pre = probe_acc[rows, :] * INV_WIDTH
        up_pre = up_acc[rows, :] * INV_WIDTH
        logistic = jax.nn.sigmoid(gate_pre)
        slope_one = logistic * (1.0 + gate_pre * (1.0 - logistic))
        slope_two = logistic * (1.0 - logistic) * (2.0 + gate_pre * (1.0 - 2.0 * logistic))
        hid[0, rows, :] = (gate_pre * logistic * up_pre).astype(bf16)
        first = up_pre * slope_one
        hid[1, rows, :] = (first * probe_pre).astype(bf16)
        gate_acc[rows, :] = first
        probe_acc[rows, :] = up_pre * slope_two * probe_pre

    target_copy.wait_recv()
    down_gather.x_forward(1)
    down_other.z_forward()

    order = (0, 1, 3, 2)

    def column(s, p):
        return mod(zh + order[s], 4) if p == 0 else lax.rem(zh + s, 4)

    def core_copy(s, p):
        return remote(core_send.at[p, s], core_recv.at[p, s], cs_s, cs_r.at[p, s], sibling)

    def forward(s, p):
        away = jnp.dot(hid[p], joined(dnb, column(s, p), 2 * (1 - core), 2), preferred_element_type=f32)
        core_send[p, s] = (away * INV_HIDDEN).astype(bf16)
        core_copy(s, p).start()
        here = jnp.dot(hid[p], joined(dnb, column(s, p), 2 * core, 2), preferred_element_type=f32)
        own_part[p, s] = here * INV_HIDDEN

    def blocks_wait(blocks, send, recv):
        return remote(blocks, blocks, send, recv, sibling)

    def rs_copy(s, p, j):
        to = lax.rem(chip + j, 8)
        return remote(
            rs_send.at[p, s, to // 4, pl.ds(pl.multiple_of(48 * lax.rem(to, 4), 48), 48)], rs_recv.at[p, s, j],
            rs_s.at[p], rs_r.at[p, s], peer(j))

    def core_sum(s, p):
        core_copy(s, p).wait_recv()
        total = own_part[p, s] + core_recv[p, s].astype(f32)
        own_part[p, s] = total
        rs_send[p, s] = total.astype(bf16).reshape(2, TOK // 2, 256)

    def scatter(s, p):
        core_sum(s, p)

        @pl.loop(1, 8)
        def _(j):
            rs_copy(s, p, j).start()

    own_rows = pl.ds(pl.multiple_of(48 * chip, 48), 48)

    def ag_copy(s, p, j):
        block = res.at[p, s, core, own_rows]
        return remote(block, block, ag_s.at[p], ag_r.at[p, s], peer(j))

    def reduce(s, p):
        blocks_wait(rs_recv.at[p, s, pl.ds(1, 7)], rs_s.at[p], rs_r.at[p, s]).wait_recv()
        total = own_part[p, s, own_rows, :]
        for j in range(1, 8):
            total = total + rs_recv[p, s, j].astype(f32)
        row = column(s, p)
        at = pl.ds(pl.multiple_of(512 * lax.rem(row, 2) + 256 * core, 256), 256)
        target = []
        for k in range(2):
            both = pair[k, :, at].astype(f32)
            target.append(jnp.where(row < 2, both[:24], both[24:]))
        total = total - jnp.concatenate(target, axis=0)
        res[p, s, core, own_rows, :] = total.astype(bf16)

        @pl.loop(1, 8)
        def _(j):
            ag_copy(s, p, j).start()

    def across_copy(s, p, k):
        return remote(res.at[p, s, k], res.at[p, s, k], ac_s, ac_r.at[p, s], sibling)

    def across(s, p):
        blocks_wait(rs_recv.at[p, s, pl.ds(1, 7)], ag_s.at[p], ag_r.at[p, s]).wait_recv()
        across_copy(s, p, core).start()

    def backward(s, p, acc):
        across_copy(s, p, 1 - core).wait_recv()
        rows = jnp.concatenate([res[p, s, 0], res[p, s, 1]], axis=1)
        part = rows_dot(joined(dnb, column(s, p), 0, 4), rows) * INV_HIDDEN
        if p == 0 and s == 0:
            acc[...] = part
        else:
            acc[...] += part

    def y_copy(s, b):
        rows = pl.ds(pl.multiple_of(48 * mod(y + b, 4), 48), 48)
        return remote(
            rs_send.at[1, s, :, rows], rs_recv.at[1, s, pl.ds(2 * b, 2)],
            rs_s.at[1], rs_r.at[1, s], same_core(0, b))

    def pair_copy(s):
        return remote(pair_send.at[s], pair_recv.at[s], pair_s, pair_r.at[s], same_core(1, 0))

    def y_scatter(s):
        core_sum(s, 1)
        for b in range(1, 4):
            y_copy(s, b).start()

    def y_reduce(s):
        blocks_wait(rs_recv.at[1, s, pl.ds(2, 6)], rs_s.at[1], rs_r.at[1, s]).wait_recv()

        def total(at):
            value = own_part[1, s, pl.ds(pl.multiple_of(48 * (4 * at + y), 48), 48), :]
            for b in range(1, 4):
                value = value + rs_recv[1, s, 2 * b + at].astype(f32)
            return value

        pair_send[s] = total(1 - half).astype(bf16)
        pair_copy(s).start()
        own_part[1, s, own_rows, :] = total(half)

    def t_copy(s, a, b):
        at = chip_at(a, 0) if b else chip
        block = res.at[1, s, core, pl.ds(pl.multiple_of(48 * at, 48), 48)]
        where = same_core(0, b) if b else same_core(1, 0)
        return remote(block, block, ag_s.at[1], ag_r.at[1, s] if b else agp_r.at[s], where)

    def pair_reduce(s):
        pair_copy(s).wait_recv()
        total = own_part[1, s, own_rows, :] + pair_recv[s].astype(f32)
        res[1, s, core, own_rows, :] = total.astype(bf16)
        t_copy(s, 1, 0).start()
        for b in range(1, 4):
            t_copy(s, 0, b).start()

    def pair_pass(s):
        t_copy(s, 1, 0).wait_recv()
        for b in range(1, 4):
            t_copy(s, 1, b).start()

    def t_across(s):
        blocks_wait(rs_recv.at[1, s, pl.ds(2, 6)], ag_s.at[1], ag_r.at[1, s]).wait_recv()
        across_copy(s, 1, core).start()

    def turn(p):
        source, turned = ((gate_acc, first_turned), (probe_acc, second_turned))[p]

        @pl.loop(0, 3)
        def _(c):
            tokens_at = pl.ds(pl.multiple_of(c * 128, 128), 128)
            turned[:, tokens_at] = source[tokens_at, :].T

    def ready(s):
        down_gather.x_last(order[s])
        if s == 3:
            down_other.z_last()

    def sums(s):
        ready(s)
        forward(s, 0)

    sums(0)
    down_gather.x_forward(3)
    sums(1)
    scatter(0, 0)
    scatter(1, 0)
    down_gather.x_forward(2)
    sums(2)
    reduce(0, 0)
    scatter(2, 0)
    sums(3)
    reduce(1, 0)
    scatter(3, 0)
    across(0, 0)
    turn(0)
    reduce(2, 0)
    backward(0, 0, grad_acc)
    across(1, 0)
    turn(1)
    reduce(3, 0)
    backward(1, 0, grad_acc)
    across(2, 0)
    backward(2, 0, grad_acc)
    across(3, 0)
    backward(3, 0, grad_acc)

    loads[4].wait()
    tang_acc[...] = jnp.zeros_like(tang_acc)

    @pl.loop(0, 7)
    def _(c):
        rows = pl.ds(pl.multiple_of(c * 64, 64), 64)
        gates[0, rows, :] = (grad_acc[rows, :] * first_turned[rows, :]).astype(bf16)

    def tangent_gates():
        @pl.loop(0, 7)
        def _(c):
            rows = pl.ds(pl.multiple_of(c * 64, 64), 64)
            gates[1, rows, :] = (
                tang_acc[rows, :] * first_turned[rows, :] + grad_acc[rows, :] * second_turned[rows, :]
            ).astype(bf16)

    tangent_steps = (
        lambda s: forward(s, 1),
        y_scatter,
        y_reduce,
        pair_reduce,
        pair_pass,
        t_across,
        lambda s: backward(s, 1, tang_acc),
    )

    def share(dest, source):
        total = jnp.int32(0)
        for k in range(6):
            total = total + jnp.where(nb_ref[k, dest] == source, num_ref[k, dest], 0)
        return total.astype(f32) * (1.0 / DEN)

    def self_share():
        total = jnp.int32(0)
        for k in range(6):
            total = total + num_ref[k, r]
        return (DEN - total).astype(f32) * (1.0 / DEN)

    loads[5].wait()
    loads[6].wait()
    sources = [replica_at(0, dx) for dx in (0, -1, 1, 2)]
    here_c = [self_share()] + [share(r, source) for source in sources[1:]]
    up_c = [share(replica_at(1, 0), source) for source in sources]
    down_c = [share(replica_at(-1, 0), source) for source in sources]

    def produce(path, pair_at):
        lanes = pl.ds(pl.multiple_of(pair_at * 256, 256), 256)
        change = jnp.dot(gates[path], x_all[:, lanes], preferred_element_type=f32) * INV_WIDTH
        old = h_ref[:, lanes].astype(f32)
        if path == 0:
            ratio = change / jnp.maximum(old, FLOOR)
            new = w_ref[:, lanes].astype(f32) - STEP_SIZE * jnp.clip(ratio, -1.0, 1.0)
        else:
            new = DECAY * old + (1.0 - DECAY) * p_ref[:, lanes].astype(f32) * change
        for m in range(2):
            own_mix[path * NC + 2 * pair_at + m] = new[:, 128 * m : 128 * (m + 1)].astype(bf16)

    def mx_copy(g, way):
        return remote(
            own_mix.at[g], (left_mix if way == 0 else right_mix).at[g],
            mx_s.at[lax.rem(g, RING), way], mx_r.at[lax.rem(g, RING), way], device(0, 1 - 2 * way))

    def mf_copy(g, way):
        part = pl.ds(way * HALF, HALF)
        return remote(
            (left_mix if way == 0 else right_mix).at[g, part], far_mix.at[g, part],
            mf_s.at[lax.rem(g, RING), way], mf_r.at[lax.rem(g, RING), way], device(0, 1 - 2 * way))

    def mz_copy(g, way):
        return remote(
            (left_mix if way == 0 else right_mix).at[g], (below if way == 0 else above).at[g],
            mz_s.at[lax.rem(g, RING), way], mz_r.at[lax.rem(g, RING), way], device(1 - 2 * way, 0))

    def x_send(g):
        @pl.when(g >= RING)
        def _():
            for way in range(2):
                mx_copy(g - RING, way).wait_send()

        for way in range(2):
            mx_copy(g, way).start()

    def x_pass(g):
        for way in range(2):
            mx_copy(g, way).wait_recv()
            mf_copy(g, way).start()

    def z_send(g):
        for way in range(2):
            mf_copy(g, way).wait_recv()
            mf_copy(g, way).wait_send()
        slot = lax.rem(g, 4)

        @pl.loop(0, 4)
        def _(piece):
            rows = pl.ds(pl.multiple_of(piece * (COLS // 4), 16), COLS // 4)
            parts = [ref[g, rows, :].astype(f32) for ref in (own_mix, left_mix, right_mix, far_mix)]

            def weighted(shares):
                total = shares[0] * parts[0]
                for c, part in zip(shares[1:], parts[1:]):
                    total = total + c * part
                return total

            mine[slot, rows, :] = weighted(here_c)
            left_mix[g, rows, :] = weighted(up_c).astype(bf16)
            right_mix[g, rows, :] = weighted(down_c).astype(bf16)

        @pl.when(g >= RING)
        def _():
            for way in range(2):
                mz_copy(g - RING, way).wait_send()

        for way in range(2):
            mz_copy(g, way).start()

    def out_copy(out, i, slot):
        return pltpu.make_async_copy(
            staged.at[slot], out.at[:, pl.ds(pl.multiple_of(i * CH, CH), CH)], out_sem.at[slot])

    def finish(out, i, g):
        for way in range(2):
            mz_copy(g, way).wait_recv()
        total = mine[lax.rem(g, 4)] + below[g].astype(f32) + above[g].astype(f32)
        slot = lax.rem(g, 2)

        @pl.when(g >= 2)
        def _():
            out_copy(out, i, slot).wait()

        staged[slot] = total.astype(bf16)
        out_copy(out, i, slot).start()

    produce(0, 0)
    x_send(0)
    produce(0, 1)
    x_send(1)
    x_pass(0)

    @pl.loop(0, 2 * NC + 2)
    def _(g):
        ahead = (g + 4) // 2

        @pl.when((lax.rem(g, 2) == 0) & (ahead < NC // 2))
        def _():
            produce(0, ahead)

        @pl.when((lax.rem(g, 2) == 0) & (ahead >= NC // 2) & (ahead < NC))
        def _():
            produce(1, ahead - NC // 2)

        @pl.when(g + 2 < 2 * NC)
        def _():
            x_send(g + 2)

        @pl.when(g + 1 < 2 * NC)
        def _():
            x_pass(g + 1)

        @pl.when(g < 2 * NC)
        def _():
            z_send(g)

        for lag, tangent_step in enumerate(tangent_steps):
            @pl.when((g >= lag) & (g < lag + 4))
            def _(lag=lag, tangent_step=tangent_step):
                tangent_step(g - lag)

        @pl.when(g == len(tangent_steps) + 3)
        def _():
            tangent_gates()

        @pl.when((g >= 2) & (g < NC + 2))
        def _():
            finish(out_w, g - 2, g - 2)

        @pl.when(g >= NC + 2)
        def _():
            finish(out_t, g - 2 - NC, g - 2)

    for slot in range(2):
        out_copy(out_t, 0, slot).wait()
    up_gather.drain()
    down_gather.drain()
    up_other.drain()
    down_other.drain()
    target_copy.wait_send()

    tk_wait(7, 0, 0).wait_send()
    tk_wait(8, 1, 0).wait_send()

    blocks_wait(rs_recv.at[0, :, pl.ds(0, 7)], rs_s.at[0], rs_r.at[0, 0]).wait_send()
    blocks_wait(rs_recv.at[0, :, pl.ds(0, 7)], ag_s.at[0], ag_r.at[0, 0]).wait_send()
    blocks_wait(rs_recv.at[1, :, pl.ds(0, 6)], rs_s.at[1], rs_r.at[1, 0]).wait_send()
    blocks_wait(rs_recv.at[1, :, pl.ds(0, 7)], ag_s.at[1], ag_r.at[1, 0]).wait_send()
    blocks_wait(pair_send, pair_s, pair_r.at[0]).wait_send()
    blocks_wait(core_send, cs_s, cs_r.at[0, 0]).wait_send()
    blocks_wait(core_send, ac_s, ac_r.at[0, 0]).wait_send()
    for g in range(2 * NC - RING, 2 * NC):
        for way in range(2):
            mx_copy(g, way).wait_send()
            mz_copy(g, way).wait_send()


PIECES = 4


def hand_on(a_ref, b_ref, a_out, b_out, held, in_sem, out_sem):
    size = COLS // PIECES
    pairs = ((a_ref, a_out), (b_ref, b_out))

    def copies(i, c):
        rows = pl.ds(c * size, size)
        inward = pltpu.make_async_copy(pairs[i][0].at[rows], held.at[i, rows], in_sem.at[i, c])
        outward = pltpu.make_async_copy(held.at[i, rows], pairs[i][1].at[rows], out_sem.at[i, c])
        return inward, outward

    every = [copies(i, c) for i in range(2) for c in range(PIECES)]
    for inward, _ in every:
        inward.start()
    for inward, outward in every:
        inward.wait()
        outward.start()
    for _, outward in every:
        outward.wait()


def local(
    tokens, targets, gate_weight, probes, tracker, up_weight, down_weight, neighbours, numerators
):
    vmem = pl.BlockSpec(memory_space=pltpu.VMEM)
    hbm = pl.BlockSpec(memory_space=pl.ANY)
    dma = pltpu.SemaphoreType.DMA
    weight = jax.ShapeDtypeStruct((COLS, D), bf16)
    wide = pltpu.VMEM((TOK, COLS), f32)
    turned = pltpu.VMEM((COLS, TOK), f32)
    mixed = pltpu.VMEM((2 * NC, COLS, CH), bf16)
    other_sems = [dma((2,)), dma((2,)), dma, dma((2,)), dma]
    gather_sems = [dma((3,)), dma((2,)), dma, dma((4, 2)), dma((4,))]
    mixed_weights, mixed_tracker = pl.pallas_call(
        kernel,
        out_shape=(weight, weight),
        in_specs=[vmem, vmem, hbm, hbm, hbm, hbm, hbm, hbm, hbm],
        out_specs=(hbm, hbm),
        scratch_shapes=[
            pltpu.SMEM((6, 16), jnp.int32),
            pltpu.SMEM((6, 16), jnp.int32),
            pltpu.VMEM((COLS, D), bf16),
            pltpu.VMEM((COLS, D), bf16),
            pltpu.VMEM((COLS, D), bf16),
            pltpu.VMEM((16, 48, 1024), bf16),
            pltpu.VMEM((2, 48, 1024), bf16),
            pltpu.VMEM((TOK, D), bf16),
            pltpu.VMEM((4, 4, COLS, 128), bf16),
            pltpu.VMEM((4, 4, COLS, 128), bf16),
            wide, wide, wide, turned, turned, turned, turned,
            pltpu.VMEM((2, TOK, COLS), bf16),
            pltpu.VMEM((2, COLS, TOK), bf16),
            pltpu.VMEM((2, 4, TOK, 256), bf16),
            pltpu.VMEM((2, 4, TOK, 256), bf16),
            pltpu.VMEM((2, 4, TOK, 256), f32),
            pltpu.VMEM((2, 4, 2, TOK // 2, 256), bf16),
            pltpu.VMEM((2, 4, 8, 48, 256), bf16),
            pltpu.VMEM((4, 48, 256), bf16),
            pltpu.VMEM((4, 48, 256), bf16),
            pltpu.VMEM((2, 4, 2, TOK, 256), bf16),
            mixed, mixed, mixed, mixed, mixed, mixed,
            pltpu.VMEM((4, COLS, CH), f32),
            pltpu.VMEM((2, COLS, CH), bf16),
            dma((7,)), dma((2,)), dma((4,)), dma, dma,
            *gather_sems, *gather_sems, *other_sems, *other_sems,
            dma, dma((2, 4)), dma((2,)), dma((2, 4)), dma, dma((4,)),
            dma((2,)), dma((2, 4)), dma((4,)), dma, dma((2, 4)),
            dma((RING, 2)), dma((RING, 2)), dma((RING, 2)), dma((RING, 2)),
            dma((RING, 2)), dma((RING, 2)), dma((2,)),
        ],
        compiler_params=pltpu.CompilerParams(
            collective_id=0, has_side_effects=True, vmem_limit_bytes=63 << 20
        ),
        name="step_and_mix",
    )(
        tokens[0], targets[0], gate_weight[0].T, probes[0].T, tracker[0].T, up_weight.T, down_weight,
        neighbours.T, numerators.T,
    )
    handed = pl.pallas_call(
        hand_on,
        out_shape=(weight, weight),
        in_specs=[hbm, hbm],
        out_specs=(hbm, hbm),
        scratch_shapes=[
            pltpu.VMEM((2, COLS, D), bf16),
            dma((2, PIECES)), dma((2, PIECES)),
        ],
        compiler_params=pltpu.CompilerParams(vmem_limit_bytes=60 << 20),
        name="hand_on",
    )(mixed_weights, mixed_tracker)
    return (handed[0].T[None], handed[1].T[None])


def solution(mesh):
    return jax.shard_map(
        local,
        mesh=mesh,
        in_specs=(
            P("replica", "tensor", None),
            P("replica", "tensor", None),
            P("replica", None, "tensor"),
            P("replica", None, "tensor"),
            P("replica", None, "tensor"),
            P("replica", "tensor"),
            P("tensor", "replica"),
            P(),
            P(),
        ),
        out_specs=(P("replica", None, "tensor"), P("replica", None, "tensor")),
        check_vma=False,
    )
```

```python
import functools
import math

import jax
import jax.numpy as jnp
from jax import lax
from jax.experimental import pallas as pl
from jax.experimental.pallas import tpu as pltpu
from jax.sharding import PartitionSpec as P

MESH = pl.DeviceIdType.MESH
D = 2048
FF = 7168
DEN = 64
TOK = 384
COLS = 448
STEP_SIZE = 0.1
FLOOR = 0.1
DECAY = 0.75
INV_WIDTH = 1.0 / math.sqrt(D)
INV_HIDDEN = 1.0 / math.sqrt(FF)

CH = 128
NC = D // CH
HALF = COLS // 2
FIRST_Z = 352
RING = 8
f32 = jnp.float32
bf16 = jnp.bfloat16


def mod(value, count):
    return lax.rem(value + 4 * count, count)


class Gather:
    first, rows = 0, FIRST_Z

    def __init__(self, ref, own, sems, zh, x, device):
        self.ref, self.own, self.zh, self.x, self.device = ref, own.at[pl.ds(self.first, self.rows)], zh, x, device
        (self.sent, self.z_r, self.zf_r, self.x_r, self.xf_r) = sems

    def slot(self, column, row):
        return self.ref.at[row, column, pl.ds(self.first, self.rows)]

    def part(self, column, row, half):
        size = self.rows // 2
        return self.ref.at[row, column, pl.ds(self.first + half * size, size)]

    def copy(self, src, dst, send, recv, dz, dx):
        return pltpu.make_async_remote_copy(
            src, dst, self.sent.at[send], recv, device_id=self.device(dz, dx), device_id_type=MESH)

    def z_copy(self, way):
        return self.copy(self.own, self.slot(self.x, self.zh), 0, self.z_r.at[way], 1 - 2 * way, 0)

    def z_start(self):
        for way in range(2):
            self.z_copy(way).start()

    def z_forward(self):
        for way in range(2):
            self.z_copy(way).wait_recv()
            block = self.part(self.x, mod(self.zh - (1 - 2 * way), 4), way)
            self.copy(block, block, 0, self.zf_r, 1 - 2 * way, 0).start()

    def whole(self, block, send, recv):
        return self.copy(block, block, send, recv, 1, 0)

    def z_last(self):
        self.whole(self.slot(self.x, mod(self.zh + 2, 4)), 0, self.zf_r).wait_recv()

    def x_copy(self, q, way):
        block = self.slot(self.x, mod(self.zh + q, 4))
        return self.copy(self.own if q == 0 else block, block, 1, self.x_r.at[q, way], 0, 1 - 2 * way)

    def x_start(self, q):
        for way in range(2):
            self.x_copy(q, way).start()

    def x_forward(self, q):
        for way in range(2):
            self.x_copy(q, way).wait_recv()
            block = self.part(mod(self.x - (1 - 2 * way), 4), mod(self.zh + q, 4), way)
            self.copy(block, block, 2, self.xf_r.at[q], 0, 1 - 2 * way).start()

    def x_last(self, q):
        self.whole(self.slot(mod(self.x + 2, 4), mod(self.zh + q, 4)), 2, self.xf_r.at[q]).wait_recv()

    def drain(self):
        rows = pl.ds(self.first, self.rows)
        sent = (self.ref.at[0, pl.ds(0, 3), rows], self.ref.at[pl.ds(0, 2), :, rows], self.ref.at[0, :, rows])
        for i, blocks in enumerate(sent):
            self.whole(blocks, i, self.zf_r).wait_send()


class RowGather(Gather):
    first, rows = FIRST_Z, COLS - FIRST_Z

    def x_copy(self, way):
        return self.copy(self.own, self.slot(self.x, self.zh), 0, self.x_r.at[way], 0, 1 - 2 * way)

    def x_start(self):
        for way in range(2):
            self.x_copy(way).start()

    def x_forward(self):
        for way in range(2):
            self.x_copy(way).wait_recv()
            block = self.part(mod(self.x - (1 - 2 * way), 4), self.zh, way)
            self.copy(block, block, 0, self.xf_r, 0, 1 - 2 * way).start()

    def x_last(self):
        self.whole(self.slot(mod(self.x + 2, 4), self.zh), 0, self.xf_r).wait_recv()

    def z_copy(self, way):
        blocks = self.ref.at[self.zh, :, pl.ds(self.first, self.rows)]
        return self.copy(blocks, blocks, 1, self.z_r.at[way], 1 - 2 * way, 0)

    def z_forward(self):
        size = self.rows // 2
        for way in range(2):
            self.z_copy(way).wait_recv()
            blocks = self.ref.at[mod(self.zh - (1 - 2 * way), 4), :, pl.ds(self.first + way * size, size)]
            self.copy(blocks, blocks, 1, self.zf_r, 1 - 2 * way, 0).start()

    def z_last(self):
        blocks = self.ref.at[mod(self.zh + 2, 4), :, pl.ds(self.first, self.rows)]
        self.whole(blocks, 1, self.zf_r).wait_recv()

    def drain(self):
        rows = pl.ds(self.first, self.rows)
        for i, blocks in enumerate((self.ref.at[0, pl.ds(0, 3), rows], self.ref.at[pl.ds(0, 3), :, rows])):
            self.whole(blocks, i, self.zf_r).wait_send()


def kernel(
    tok_ref, tgt_ref, w_hbm, p_hbm, h_hbm, up_ref, down_ref, nb_hbm, num_hbm,
    out_w, out_t,
    nb_ref, num_ref,
    w_ref, p_ref, h_ref, tk, pair, x_all, upb, dnb,
    gate_acc, probe_acc, up_acc, first_turned, second_turned, grad_acc, tang_acc,
    hid, gates, core_send, core_recv, own_part, rs_send, rs_recv, pair_send, pair_recv, res,
    own_mix, left_mix, right_mix, far_mix, below, above, mine, staged,
    load_sem, tk_s, tk_r, tg_s, tg_r,
    u_s, uz_r, uzf_r, ux_r, uxf_r,
    d_s, dz_r, dzf_r, dx_r, dxf_r,
    ru_s, ruz_r, ruzf_r, rux_r, ruxf_r,
    rd_s, rdz_r, rdzf_r, rdx_r, rdxf_r,
    cs_s, cs_r, rs_s, rs_r, pair_s, pair_r, ag_s, ag_r, agp_r, ac_s, ac_r,
    mx_s, mx_r, mf_s, mf_r, mz_s, mz_r, out_sem,
):
    r = lax.axis_index("replica")
    t = lax.axis_index("tensor")
    zh, x = r // 4, lax.rem(r, 4)
    chip, core = t // 2, lax.rem(t, 2)
    half, y = chip // 4, lax.rem(chip, 4)
    sibling = (r, 2 * chip + 1 - core)

    def replica_at(dz, dx):
        return mod(zh + dz, 4) * 4 + mod(x + dx, 4)

    def device(dz, dx):
        return (replica_at(dz, dx), t)

    def peer(j):
        return (r, 2 * lax.rem(chip + j, 8) + core)

    def chip_at(a, b):
        return 4 * lax.rem(half + a, 2) + mod(y + b, 4)

    def same_core(a, b):
        return (r, 2 * chip_at(a, b) + core)

    def remote(src, dst, send, recv, where):
        return pltpu.make_async_remote_copy(
            src, dst, send, recv, device_id=where, device_id_type=MESH)

    barrier = pltpu.get_barrier_semaphore()
    partners = [device(1, 0), device(-1, 0), device(0, 1), device(0, -1), sibling]
    for where in partners:
        pl.semaphore_signal(barrier, inc=1, device_id=where, device_id_type=MESH)

    @pl.loop(1, 8)
    def _(j):
        pl.semaphore_signal(barrier, inc=1, device_id=peer(j), device_id_type=MESH)

    locals_in = (
        (up_ref, upb.at[zh, x]), (down_ref, dnb.at[zh, x]), (w_hbm, w_ref), (p_hbm, p_ref),
        (h_hbm, h_ref), (nb_hbm, nb_ref), (num_hbm, num_ref),
    )
    loads = [
        pltpu.make_async_copy(src, dst, load_sem.at[i]) for i, (src, dst) in enumerate(locals_in)
    ]
    for load in loads:
        load.start()

    def packed_rows(ref):
        block = ref[...].astype(f32)
        return jnp.concatenate([block[:, :1024], block[:, 1024:]], axis=0).astype(bf16)

    tk[t] = packed_rows(tok_ref)
    pair[core] = packed_rows(tgt_ref)
    pl.semaphore_wait(barrier, 12)

    def tk_slot(a, b):
        return tk.at[2 * chip_at(a, b) + core]

    def tk_copy(a, b):
        block = tk_slot(a, 0) if b else tk_slot(0, 0)
        where = same_core(0, b) if b else same_core(1, 0)
        return remote(block, block, tk_s.at[0], tk_r.at[2 * a + (b > 0)], where)

    def tk_pass(a, b):
        block = tk_slot(a, -b)
        return remote(block, block, tk_s.at[1], tk_r.at[0], sibling)

    def tk_wait(count, send, recv):
        return remote(tk.at[pl.ds(0, count)], tk.at[pl.ds(0, count)], tk_s.at[send], tk_r.at[recv], sibling)

    target_copy = remote(pair.at[core], pair.at[core], tg_s, tg_r, sibling)

    up_gather = Gather(upb, up_ref, (u_s, uz_r, uzf_r, ux_r, uxf_r), zh, x, device)
    down_gather = Gather(dnb, down_ref, (d_s, dz_r, dzf_r, dx_r, dxf_r), zh, x, device)
    up_other = RowGather(upb, up_ref, (ru_s, ruz_r, ruzf_r, rux_r, ruxf_r), zh, x, device)
    down_other = RowGather(dnb, down_ref, (rd_s, rdz_r, rdzf_r, rdx_r, rdxf_r), zh, x, device)

    tk_copy(1, 0).start()
    for b in range(1, 4):
        tk_copy(0, b).start()
    up_gather.z_start()
    up_other.x_start()
    up_gather.x_start(0)
    tk_pass(0, 0).start()
    target_copy.start()

    tk_copy(1, 0).wait_recv()
    for b in range(1, 4):
        tk_copy(1, b).start()
    tk_pass(1, 0).start()
    up_other.x_forward()
    down_other.x_start()
    down_gather.x_start(0)
    up_gather.x_forward(0)
    up_gather.z_forward()
    up_gather.x_start(1)
    up_gather.x_start(3)
    loads[0].wait()
    up_other.x_last()
    up_other.z_start()
    down_other.x_forward()
    tk_wait(3, 0, 1).wait_recv()
    for b in range(1, 4):
        tk_pass(0, b).start()
    up_gather.z_last()
    up_gather.x_start(2)
    down_gather.z_start()
    down_gather.x_forward(0)
    tk_wait(3, 0, 3).wait_recv()
    for b in range(1, 4):
        tk_pass(1, b).start()
    up_gather.x_forward(1)
    tk_wait(8, 1, 0).wait_recv()

    @pl.loop(0, 8)
    def _(c):
        blocks = [tk[2 * c + k].astype(f32) for k in range(2)]
        rows = [jnp.concatenate([b[:24], b[24:]], axis=1) for b in blocks]
        x_all[pl.ds(pl.multiple_of(c * 48, 48), 48), :] = jnp.concatenate(rows, axis=0).astype(bf16)

    up_gather.x_forward(3)
    up_other.z_forward()

    def joined(ref, row, first, count):
        return jnp.concatenate([ref[row, first + i] for i in range(count)], axis=1)

    def rows_dot(left, right):
        return lax.dot_general(left, right, (((1,), (1,)), ((), ())), preferred_element_type=f32)

    def wide_dot(acc, weight):
        acc[...] = rows_dot(x_all[...], weight[...])

    loads[2].wait()
    wide_dot(gate_acc, w_ref)
    up_gather.x_forward(2)
    down_gather.z_forward()
    down_gather.x_start(1)
    down_gather.x_start(3)
    loads[1].wait()
    down_other.x_last()
    down_other.z_start()
    loads[3].wait()
    wide_dot(probe_acc, p_ref)

    def up_rows(q):
        row = mod(zh + q, 4)
        return rows_dot(x_all[:, pl.ds(pl.multiple_of(512 * row, 512), 512)], joined(upb, row, 0, 4))

    for q in (0, 1, 3):
        up_gather.x_last(q)
    up_other.z_last()
    up_acc[...] = up_rows(0) + up_rows(1) + up_rows(3)
    up_gather.x_last(2)
    up_acc[...] += up_rows(2)
    down_gather.z_last()
    down_gather.x_start(2)

    @pl.loop(0, 8)
    def _(c):
        rows = pl.ds(pl.multiple_of(c * 48, 48), 48)
        gate_pre = gate_acc[rows, :] * INV_WIDTH
        probe_pre = probe_acc[rows, :] * INV_WIDTH
        up_pre = up_acc[rows, :] * INV_WIDTH
        logistic = jax.nn.sigmoid(gate_pre)
        slope_one = logistic * (1.0 + gate_pre * (1.0 - logistic))
        slope_two = logistic * (1.0 - logistic) * (2.0 + gate_pre * (1.0 - 2.0 * logistic))
        hid[0, rows, :] = (gate_pre * logistic * up_pre).astype(bf16)
        first = up_pre * slope_one
        hid[1, rows, :] = (first * probe_pre).astype(bf16)
        gate_acc[rows, :] = first
        probe_acc[rows, :] = up_pre * slope_two * probe_pre

    target_copy.wait_recv()
    down_gather.x_forward(1)
    down_other.z_forward()

    order = (0, 1, 3, 2)

    def column(s, p):
        return mod(zh + order[s], 4) if p == 0 else lax.rem(zh + s, 4)

    def core_copy(s, p):
        return remote(core_send.at[p, s], core_recv.at[p, s], cs_s, cs_r.at[p, s], sibling)

    def forward(s, p):
        away = jnp.dot(hid[p], joined(dnb, column(s, p), 2 * (1 - core), 2), preferred_element_type=f32)
        core_send[p, s] = (away * INV_HIDDEN).astype(bf16)
        core_copy(s, p).start()
        here = jnp.dot(hid[p], joined(dnb, column(s, p), 2 * core, 2), preferred_element_type=f32)
        own_part[p, s] = here * INV_HIDDEN

    def blocks_wait(blocks, send, recv):
        return remote(blocks, blocks, send, recv, sibling)

    def rs_copy(s, p, j):
        to = lax.rem(chip + j, 8)
        return remote(
            rs_send.at[p, s, to // 4, pl.ds(pl.multiple_of(48 * lax.rem(to, 4), 48), 48)], rs_recv.at[p, s, j],
            rs_s.at[p], rs_r.at[p, s], peer(j))

    def core_sum(s, p):
        core_copy(s, p).wait_recv()
        total = own_part[p, s] + core_recv[p, s].astype(f32)
        own_part[p, s] = total
        rs_send[p, s] = total.astype(bf16).reshape(2, TOK // 2, 256)

    def scatter(s, p):
        core_sum(s, p)

        @pl.loop(1, 8)
        def _(j):
            rs_copy(s, p, j).start()

    own_rows = pl.ds(pl.multiple_of(48 * chip, 48), 48)

    def ag_copy(s, p, j):
        block = res.at[p, s, core, own_rows]
        return remote(block, block, ag_s.at[p], ag_r.at[p, s], peer(j))

    def reduce(s, p):
        blocks_wait(rs_recv.at[p, s, pl.ds(1, 7)], rs_s.at[p], rs_r.at[p, s]).wait_recv()
        total = own_part[p, s, own_rows, :]
        for j in range(1, 8):
            total = total + rs_recv[p, s, j].astype(f32)
        row = column(s, p)
        at = pl.ds(pl.multiple_of(512 * lax.rem(row, 2) + 256 * core, 256), 256)
        target = []
        for k in range(2):
            both = pair[k, :, at].astype(f32)
            target.append(jnp.where(row < 2, both[:24], both[24:]))
        total = total - jnp.concatenate(target, axis=0)
        res[p, s, core, own_rows, :] = total.astype(bf16)

        @pl.loop(1, 8)
        def _(j):
            ag_copy(s, p, j).start()

    def across_copy(s, p, k):
        return remote(res.at[p, s, k], res.at[p, s, k], ac_s, ac_r.at[p, s], sibling)

    def across(s, p):
        blocks_wait(rs_recv.at[p, s, pl.ds(1, 7)], ag_s.at[p], ag_r.at[p, s]).wait_recv()
        across_copy(s, p, core).start()

    def backward(s, p, acc):
        across_copy(s, p, 1 - core).wait_recv()
        rows = jnp.concatenate([res[p, s, 0], res[p, s, 1]], axis=1)
        part = rows_dot(joined(dnb, column(s, p), 0, 4), rows) * INV_HIDDEN
        if p == 0 and s == 0:
            acc[...] = part
        else:
            acc[...] += part

    def y_copy(s, b):
        rows = pl.ds(pl.multiple_of(48 * mod(y + b, 4), 48), 48)
        return remote(
            rs_send.at[1, s, :, rows], rs_recv.at[1, s, pl.ds(2 * b, 2)],
            rs_s.at[1], rs_r.at[1, s], same_core(0, b))

    def pair_copy(s):
        return remote(pair_send.at[s], pair_recv.at[s], pair_s, pair_r.at[s], same_core(1, 0))

    def y_scatter(s):
        core_sum(s, 1)
        for b in range(1, 4):
            y_copy(s, b).start()

    def y_reduce(s):
        blocks_wait(rs_recv.at[1, s, pl.ds(2, 6)], rs_s.at[1], rs_r.at[1, s]).wait_recv()

        def total(at):
            value = own_part[1, s, pl.ds(pl.multiple_of(48 * (4 * at + y), 48), 48), :]
            for b in range(1, 4):
                value = value + rs_recv[1, s, 2 * b + at].astype(f32)
            return value

        pair_send[s] = total(1 - half).astype(bf16)
        pair_copy(s).start()
        own_part[1, s, own_rows, :] = total(half)

    def t_copy(s, a, b):
        at = chip_at(a, 0) if b else chip
        block = res.at[1, s, core, pl.ds(pl.multiple_of(48 * at, 48), 48)]
        where = same_core(0, b) if b else same_core(1, 0)
        return remote(block, block, ag_s.at[1], ag_r.at[1, s] if b else agp_r.at[s], where)

    def pair_reduce(s):
        pair_copy(s).wait_recv()
        total = own_part[1, s, own_rows, :] + pair_recv[s].astype(f32)
        res[1, s, core, own_rows, :] = total.astype(bf16)
        t_copy(s, 1, 0).start()
        for b in range(1, 4):
            t_copy(s, 0, b).start()

    def pair_pass(s):
        t_copy(s, 1, 0).wait_recv()
        for b in range(1, 4):
            t_copy(s, 1, b).start()

    def t_across(s):
        blocks_wait(rs_recv.at[1, s, pl.ds(2, 6)], ag_s.at[1], ag_r.at[1, s]).wait_recv()
        across_copy(s, 1, core).start()

    def turn(p):
        source, turned = ((gate_acc, first_turned), (probe_acc, second_turned))[p]

        @pl.loop(0, 3)
        def _(c):
            tokens_at = pl.ds(pl.multiple_of(c * 128, 128), 128)
            turned[:, tokens_at] = source[tokens_at, :].T

    def ready(s):
        down_gather.x_last(order[s])
        if s == 3:
            down_other.z_last()

    def sums(s):
        ready(s)
        forward(s, 0)

    sums(0)
    down_gather.x_forward(3)
    sums(1)
    scatter(0, 0)
    scatter(1, 0)
    down_gather.x_forward(2)
    sums(2)
    reduce(0, 0)
    scatter(2, 0)
    sums(3)
    reduce(1, 0)
    scatter(3, 0)
    across(0, 0)
    turn(0)
    reduce(2, 0)
    backward(0, 0, grad_acc)
    across(1, 0)
    turn(1)
    reduce(3, 0)
    backward(1, 0, grad_acc)
    across(2, 0)
    backward(2, 0, grad_acc)
    across(3, 0)
    backward(3, 0, grad_acc)

    loads[4].wait()
    tang_acc[...] = jnp.zeros_like(tang_acc)

    @pl.loop(0, 7)
    def _(c):
        rows = pl.ds(pl.multiple_of(c * 64, 64), 64)
        gates[0, rows, :] = (grad_acc[rows, :] * first_turned[rows, :]).astype(bf16)

    def tangent_gates():
        @pl.loop(0, 7)
        def _(c):
            rows = pl.ds(pl.multiple_of(c * 64, 64), 64)
            gates[1, rows, :] = (
                tang_acc[rows, :] * first_turned[rows, :] + grad_acc[rows, :] * second_turned[rows, :]
            ).astype(bf16)

    tangent_steps = (
        lambda s: forward(s, 1),
        y_scatter,
        y_reduce,
        pair_reduce,
        pair_pass,
        t_across,
        lambda s: backward(s, 1, tang_acc),
    )

    def share(dest, source):
        total = jnp.int32(0)
        for k in range(6):
            total = total + jnp.where(nb_ref[k, dest] == source, num_ref[k, dest], 0)
        return total.astype(f32) * (1.0 / DEN)

    def self_share():
        total = jnp.int32(0)
        for k in range(6):
            total = total + num_ref[k, r]
        return (DEN - total).astype(f32) * (1.0 / DEN)

    loads[5].wait()
    loads[6].wait()
    sources = [replica_at(0, dx) for dx in (0, -1, 1, 2)]
    here_c = [self_share()] + [share(r, source) for source in sources[1:]]
    up_c = [share(replica_at(1, 0), source) for source in sources]
    down_c = [share(replica_at(-1, 0), source) for source in sources]

    def produce(path, pair_at):
        lanes = pl.ds(pl.multiple_of(pair_at * 256, 256), 256)
        change = jnp.dot(gates[path], x_all[:, lanes], preferred_element_type=f32) * INV_WIDTH
        old = h_ref[:, lanes].astype(f32)
        if path == 0:
            ratio = change / jnp.maximum(old, FLOOR)
            new = w_ref[:, lanes].astype(f32) - STEP_SIZE * jnp.clip(ratio, -1.0, 1.0)
        else:
            new = DECAY * old + (1.0 - DECAY) * p_ref[:, lanes].astype(f32) * change
        for m in range(2):
            own_mix[path * NC + 2 * pair_at + m] = new[:, 128 * m : 128 * (m + 1)].astype(bf16)

    def mx_copy(g, way):
        return remote(
            own_mix.at[g], (left_mix if way == 0 else right_mix).at[g],
            mx_s.at[lax.rem(g, RING), way], mx_r.at[lax.rem(g, RING), way], device(0, 1 - 2 * way))

    def mf_copy(g, way):
        part = pl.ds(way * HALF, HALF)
        return remote(
            (left_mix if way == 0 else right_mix).at[g, part], far_mix.at[g, part],
            mf_s.at[lax.rem(g, RING), way], mf_r.at[lax.rem(g, RING), way], device(0, 1 - 2 * way))

    def mz_copy(g, way):
        return remote(
            (left_mix if way == 0 else right_mix).at[g], (below if way == 0 else above).at[g],
            mz_s.at[lax.rem(g, RING), way], mz_r.at[lax.rem(g, RING), way], device(1 - 2 * way, 0))

    def x_send(g):
        @pl.when(g >= RING)
        def _():
            for way in range(2):
                mx_copy(g - RING, way).wait_send()

        for way in range(2):
            mx_copy(g, way).start()

    def x_pass(g):
        for way in range(2):
            mx_copy(g, way).wait_recv()
            mf_copy(g, way).start()

    def z_send(g):
        for way in range(2):
            mf_copy(g, way).wait_recv()
            mf_copy(g, way).wait_send()
        slot = lax.rem(g, 4)

        @pl.loop(0, 4)
        def _(piece):
            rows = pl.ds(pl.multiple_of(piece * (COLS // 4), 16), COLS // 4)
            parts = [ref[g, rows, :].astype(f32) for ref in (own_mix, left_mix, right_mix, far_mix)]

            def weighted(shares):
                total = shares[0] * parts[0]
                for c, part in zip(shares[1:], parts[1:]):
                    total = total + c * part
                return total

            mine[slot, rows, :] = weighted(here_c)
            left_mix[g, rows, :] = weighted(up_c).astype(bf16)
            right_mix[g, rows, :] = weighted(down_c).astype(bf16)

        @pl.when(g >= RING)
        def _():
            for way in range(2):
                mz_copy(g - RING, way).wait_send()

        for way in range(2):
            mz_copy(g, way).start()

    def out_copy(out, i, slot):
        return pltpu.make_async_copy(
            staged.at[slot], out.at[:, pl.ds(pl.multiple_of(i * CH, CH), CH)], out_sem.at[slot])

    def finish(out, i, g):
        for way in range(2):
            mz_copy(g, way).wait_recv()
        total = mine[lax.rem(g, 4)] + below[g].astype(f32) + above[g].astype(f32)
        slot = lax.rem(g, 2)

        @pl.when(g >= 2)
        def _():
            out_copy(out, i, slot).wait()

        staged[slot] = total.astype(bf16)
        out_copy(out, i, slot).start()

    produce(0, 0)
    x_send(0)
    produce(0, 1)
    x_pass(0)
    x_send(1)

    @pl.loop(0, 2 * NC + 2)
    def _(g):
        ahead = (g + 4) // 2

        @pl.when((lax.rem(g, 2) == 0) & (ahead < NC // 2))
        def _():
            produce(0, ahead)

        @pl.when((lax.rem(g, 2) == 0) & (ahead >= NC // 2) & (ahead < NC))
        def _():
            produce(1, ahead - NC // 2)

        @pl.when(g + 2 < 2 * NC)
        def _():
            x_send(g + 2)

        @pl.when(g + 1 < 2 * NC)
        def _():
            x_pass(g + 1)

        @pl.when(g < 2 * NC)
        def _():
            z_send(g)

        for lag, tangent_step in enumerate(tangent_steps):
            @pl.when((g >= lag) & (g < lag + 4))
            def _(lag=lag, tangent_step=tangent_step):
                tangent_step(g - lag)

        @pl.when(g == len(tangent_steps) + 3)
        def _():
            tangent_gates()

        @pl.when((g >= 2) & (g < NC + 2))
        def _():
            finish(out_w, g - 2, g - 2)

        @pl.when(g >= NC + 2)
        def _():
            finish(out_t, g - 2 - NC, g - 2)

    for slot in range(2):
        out_copy(out_t, 0, slot).wait()
    up_gather.drain()
    down_gather.drain()
    up_other.drain()
    down_other.drain()
    target_copy.wait_send()

    tk_wait(7, 0, 0).wait_send()
    tk_wait(8, 1, 0).wait_send()

    blocks_wait(rs_recv.at[0, :, pl.ds(0, 7)], rs_s.at[0], rs_r.at[0, 0]).wait_send()
    blocks_wait(rs_recv.at[0, :, pl.ds(0, 7)], ag_s.at[0], ag_r.at[0, 0]).wait_send()
    blocks_wait(rs_recv.at[1, :, pl.ds(0, 6)], rs_s.at[1], rs_r.at[1, 0]).wait_send()
    blocks_wait(rs_recv.at[1, :, pl.ds(0, 7)], ag_s.at[1], ag_r.at[1, 0]).wait_send()
    blocks_wait(pair_send, pair_s, pair_r.at[0]).wait_send()
    blocks_wait(core_send, cs_s, cs_r.at[0, 0]).wait_send()
    blocks_wait(core_send, ac_s, ac_r.at[0, 0]).wait_send()
    for g in range(2 * NC - RING, 2 * NC):
        for way in range(2):
            mx_copy(g, way).wait_send()
            mz_copy(g, way).wait_send()


PIECES = 4


def hand_on(a_ref, b_ref, a_out, b_out, held, in_sem, out_sem):
    size = COLS // PIECES
    pairs = ((a_ref, a_out), (b_ref, b_out))

    def copies(i, c):
        rows = pl.ds(c * size, size)
        inward = pltpu.make_async_copy(pairs[i][0].at[rows], held.at[i, rows], in_sem.at[i, c])
        outward = pltpu.make_async_copy(held.at[i, rows], pairs[i][1].at[rows], out_sem.at[i, c])
        return inward, outward

    every = [copies(i, c) for i in range(2) for c in range(PIECES)]
    for inward, _ in every:
        inward.start()
    for inward, outward in every:
        inward.wait()
        outward.start()
    for _, outward in every:
        outward.wait()


def local(
    tokens, targets, gate_weight, probes, tracker, up_weight, down_weight, neighbours, numerators
):
    vmem = pl.BlockSpec(memory_space=pltpu.VMEM)
    hbm = pl.BlockSpec(memory_space=pl.ANY)
    dma = pltpu.SemaphoreType.DMA
    weight = jax.ShapeDtypeStruct((COLS, D), bf16)
    wide = pltpu.VMEM((TOK, COLS), f32)
    turned = pltpu.VMEM((COLS, TOK), f32)
    mixed = pltpu.VMEM((2 * NC, COLS, CH), bf16)
    other_sems = [dma((2,)), dma((2,)), dma, dma((2,)), dma]
    gather_sems = [dma((3,)), dma((2,)), dma, dma((4, 2)), dma((4,))]
    mixed_weights, mixed_tracker = pl.pallas_call(
        kernel,
        out_shape=(weight, weight),
        in_specs=[vmem, vmem, hbm, hbm, hbm, hbm, hbm, hbm, hbm],
        out_specs=(hbm, hbm),
        scratch_shapes=[
            pltpu.SMEM((6, 16), jnp.int32),
            pltpu.SMEM((6, 16), jnp.int32),
            pltpu.VMEM((COLS, D), bf16),
            pltpu.VMEM((COLS, D), bf16),
            pltpu.VMEM((COLS, D), bf16),
            pltpu.VMEM((16, 48, 1024), bf16),
            pltpu.VMEM((2, 48, 1024), bf16),
            pltpu.VMEM((TOK, D), bf16),
            pltpu.VMEM((4, 4, COLS, 128), bf16),
            pltpu.VMEM((4, 4, COLS, 128), bf16),
            wide, wide, wide, turned, turned, turned, turned,
            pltpu.VMEM((2, TOK, COLS), bf16),
            pltpu.VMEM((2, COLS, TOK), bf16),
            pltpu.VMEM((2, 4, TOK, 256), bf16),
            pltpu.VMEM((2, 4, TOK, 256), bf16),
            pltpu.VMEM((2, 4, TOK, 256), f32),
            pltpu.VMEM((2, 4, 2, TOK // 2, 256), bf16),
            pltpu.VMEM((2, 4, 8, 48, 256), bf16),
            pltpu.VMEM((4, 48, 256), bf16),
            pltpu.VMEM((4, 48, 256), bf16),
            pltpu.VMEM((2, 4, 2, TOK, 256), bf16),
            mixed, mixed, mixed, mixed, mixed, mixed,
            pltpu.VMEM((4, COLS, CH), f32),
            pltpu.VMEM((2, COLS, CH), bf16),
            dma((7,)), dma((2,)), dma((4,)), dma, dma,
            *gather_sems, *gather_sems, *other_sems, *other_sems,
            dma, dma((2, 4)), dma((2,)), dma((2, 4)), dma, dma((4,)),
            dma((2,)), dma((2, 4)), dma((4,)), dma, dma((2, 4)),
            dma((RING, 2)), dma((RING, 2)), dma((RING, 2)), dma((RING, 2)),
            dma((RING, 2)), dma((RING, 2)), dma((2,)),
        ],
        compiler_params=pltpu.CompilerParams(
            collective_id=0, has_side_effects=True, vmem_limit_bytes=63 << 20
        ),
        name="step_and_mix",
    )(
        tokens[0], targets[0], gate_weight[0].T, probes[0].T, tracker[0].T, up_weight.T, down_weight,
        neighbours.T, numerators.T,
    )
    handed = pl.pallas_call(
        hand_on,
        out_shape=(weight, weight),
        in_specs=[hbm, hbm],
        out_specs=(hbm, hbm),
        scratch_shapes=[
            pltpu.VMEM((2, COLS, D), bf16),
            dma((2, PIECES)), dma((2, PIECES)),
        ],
        compiler_params=pltpu.CompilerParams(vmem_limit_bytes=60 << 20),
        name="hand_on",
    )(mixed_weights, mixed_tracker)
    return (handed[0].T[None], handed[1].T[None])


def solution(mesh):
    return jax.shard_map(
        local,
        mesh=mesh,
        in_specs=(
            P("replica", "tensor", None),
            P("replica", "tensor", None),
            P("replica", None, "tensor"),
            P("replica", None, "tensor"),
            P("replica", None, "tensor"),
            P("replica", "tensor"),
            P("tensor", "replica"),
            P(),
            P(),
        ),
        out_specs=(P("replica", None, "tensor"), P("replica", None, "tensor")),
        check_vma=False,
    )
```
